256 devices in a mesh: seq: 32 (over z, y), tp: 8 (over x, core).
Axes of the slice: x: 4, y: 4, z: 8, core: 2. Of those that a mesh axis runs over, the one named last changes fastest.
Arguments:
- queries: bfloat16 [1024, 8192], P('seq', 'tp'), may hold values from -6 to 6
- prefix_keys: bfloat16 [32768, 1024], P('seq', 'tp'), may hold values from -10 to 10
- prefix_values: bfloat16 [32768, 1024], P('seq', 'tp'), may hold values from -6 to 6
- new_keys: bfloat16 [1024, 1024], P('seq', 'tp'), may hold values from -10 to 10
- new_values: bfloat16 [1024, 1024], P('seq', 'tp'), may hold values from -6 to 6
- cache_keys: bfloat16 [128, 512, 1024], P('seq', None, 'tp'), may hold values from -14 to 14
- cache_values: bfloat16 [128, 512, 1024], P('seq', None, 'tp'), may hold values from -6 to 6
- row_request: int32 [1024], P('seq'), may hold values from 0 to 127, as said below
- cache_lengths: int32 [128], P('seq'), may hold values from 1 to 512
- out_weight: bfloat16 [8192, 8192], P('tp', 'seq'), may hold values from -0.25 to 0.25
Outputs:
- projected: bfloat16 [1024, 8192], P('tp', 'seq')
The draws below stay inside these ranges and needn't reach their ends.
Inputs may be any that keep to these rules, and one draw needn't show every extreme that they name: `row_request`: the rows of one request stand together on the index of seq that owns the request (requests s * 4 to s * 4 + 3 own rows s * 32 to s * 32 + 31), in order of position; each owner's first row belongs to its first request and its last row to its last.
All inputs are finite; a program needn't handle non-finite values.
Results may differ from the reference program's by a relative error of at most 0.019.
Values may be sent and summed in bfloat16 or wider, within the bound.
A program may use at most 320 MiB of HBM per device.

```python
import math
import jax
import jax.numpy as jnp
from jax import lax

D = 8192
HEADS = 64
KVH = 8
HD = 128
QPG = 8
PREFIX_DEV = 1024
PREFIX = 32768
ROW_DEV = 32
ROWS = 1024
REQ_DEV = 4
REQS = 128
SUF = 512
N_SEQ = 32


def draw_queries(key, part):
    key = jax.random.fold_in(key, 11)
    values = jnp.clip(jax.random.normal(key, (ROWS, HEADS * HD), jnp.float32), -6.0, 6.0)
    return values.astype(jnp.bfloat16)


def draw_prefix_keys(key, part):
    key = jax.random.fold_in(key, 23)
    values = jnp.clip(2.5 * jax.random.normal(key, (PREFIX, KVH * HD), jnp.float32), -10.0, 10.0)
    return values.astype(jnp.bfloat16)


def draw_row_request(key, part):
    key = jax.random.fold_in(key, 37)
    owners = ROWS // ROW_DEV
    picks = jnp.sort(jax.random.randint(key, (owners, ROW_DEV), 0, REQ_DEV), axis=1)
    picks = picks.at[:, 0].set(0).at[:, ROW_DEV - 1].set(REQ_DEV - 1)
    picks = picks + jnp.arange(owners, dtype=jnp.int32)[:, None] * REQ_DEV
    return picks.reshape(ROWS).astype(jnp.int32)


def draw_cache_lengths(key, part):
    key = jax.random.fold_in(key, 53)
    counts = jax.random.randint(key, (REQS,), 1, SUF + 1)
    counts = counts.at[0].set(SUF).at[1].set(1)
    return counts.astype(jnp.int32)


def levels(rng, shape, split, low, top_value):
    gain = 1.0
    for dim, blocks in split:
        draws = jax.random.uniform(jax.random.fold_in(jax.random.fold_in(rng, 6), dim), (blocks,), jnp.float32, low / len(split), top_value / len(split))
        gain = gain * jnp.repeat(jnp.exp(draws), shape[dim] // blocks).reshape((-1,) + (1,) * (len(shape) - 1 - dim))
    return gain


def gaussian(key, shape, spread, reach, shards=(), kind=jnp.bfloat16):
    gain = levels(key, shape, shards, -0.22, 0.18) if shards else 1.0
    values = jax.random.normal(key, shape, jnp.float32) * spread * gain
    return jnp.minimum(jnp.maximum(values, -reach), reach).astype(kind)


def setup_inputs(seed: int = 0) -> dict:
    keys = jax.random.split(jax.random.key(seed), 11)
    return {
        "queries": draw_queries(jax.random.fold_in(keys[10], 71), 0),
        "prefix_keys": draw_prefix_keys(jax.random.fold_in(keys[10], 71), 0),
        "prefix_values": gaussian(keys[2], (PREFIX, KVH * HD), 1.0, 6.0, ((0, 32), (1, 8))),
        "new_keys": gaussian(keys[3], (ROWS, KVH * HD), 2.5, 10.0, ((0, 32), (1, 8))),
        "new_values": gaussian(keys[4], (ROWS, KVH * HD), 1.0, 6.0, ((0, 32), (1, 8))),
        "cache_keys": gaussian(keys[5], (REQS, SUF, KVH * HD), 3.5, 14.0, ((0, 32), (2, 8))),
        "cache_values": gaussian(keys[6], (REQS, SUF, KVH * HD), 1.0, 6.0, ((0, 32), (2, 8))),
        "row_request": draw_row_request(jax.random.fold_in(keys[10], 71), 0),
        "cache_lengths": draw_cache_lengths(jax.random.fold_in(keys[10], 71), 0),
        "out_weight": gaussian(keys[9], (HEADS * HD, D), (HEADS * HD // 16) ** -0.5, 0.25, ((0, 8), (1, 32))),
    }


def reference(queries, prefix_keys, prefix_values, new_keys, new_values, cache_keys, cache_values, row_request, cache_lengths, out_weight):
    inv_root = 1.0 / math.sqrt(HD)
    block_rows = math.gcd(ROWS, 128)
    block_count = ROWS // block_rows
    positions = jnp.arange(ROWS, dtype=jnp.int32)
    slot_index = jnp.arange(SUF, dtype=jnp.int32)
    running_highest = lax.Precision.HIGHEST

    def head_group(group_idx):
        col_first = (group_idx * HD).astype(jnp.int32)
        pre_keys = lax.dynamic_slice_in_dim(prefix_keys, col_first, HD, 1).astype(jnp.float32)
        prefix_value_rows = lax.dynamic_slice_in_dim(prefix_values, col_first, HD, 1).astype(jnp.float32).reshape(N_SEQ, PREFIX_DEV, HD)
        row_keys = lax.dynamic_slice_in_dim(new_keys, col_first, HD, 1).astype(jnp.float32)
        row_values = lax.dynamic_slice_in_dim(new_values, col_first, HD, 1).astype(jnp.float32)
        suffix_keys = lax.dynamic_slice_in_dim(cache_keys, col_first, HD, 2)
        suf_values = lax.dynamic_slice_in_dim(cache_values, col_first, HD, 2)
        query_cols = lax.dynamic_slice_in_dim(queries, (group_idx * QPG * HD).astype(jnp.int32), QPG * HD, 1)

        def one_block(block_idx):
            first_row = (block_idx * block_rows).astype(jnp.int32)
            query = lax.dynamic_slice_in_dim(query_cols, first_row, block_rows, 0).astype(jnp.float32).reshape(block_rows, QPG, HD)
            requests = lax.dynamic_slice_in_dim(row_request, first_row, block_rows, 0)
            row_pos = first_row + jnp.arange(block_rows, dtype=jnp.int32)
            own_keys = suffix_keys[requests].astype(jnp.float32)
            own_values = suf_values[requests].astype(jnp.float32)
            own_lengths = cache_lengths[requests]
            pre_scores = jnp.einsum('rqd,kd->rqk', query, pre_keys, precision=running_highest) * inv_root
            pre_scores = pre_scores.reshape(block_rows, QPG, N_SEQ, PREFIX_DEV)
            block_max = pre_scores.max(-1)
            block_exps = jnp.exp(pre_scores - block_max[..., None])
            block_total = block_exps.sum(-1)
            block_weight_total = lax.optimization_barrier(block_exps.astype(jnp.bfloat16)).astype(jnp.float32)
            block_exp_sum = jnp.einsum('fany,nye->fane', block_weight_total, prefix_value_rows, precision=running_highest)
            part_out = lax.optimization_barrier((block_exp_sum / block_total[..., None]).astype(jnp.bfloat16)).astype(jnp.float32)
            part_lse = block_max + jnp.log(block_total)
            suf_scores = jnp.einsum('rqd,rkd->rqk', query, own_keys, precision=running_highest) * inv_root
            new_scores = jnp.einsum('rqd,kd->rqk', query, row_keys, precision=running_highest) * inv_root
            suf_usable = (slot_index[None, :] < own_lengths[:, None])[:, None, :]
            new_usable = ((requests[:, None] == row_request[None, :]) & (positions[None, :] <= row_pos[:, None]))[:, None, :]
            suf_scores = jnp.where(suf_usable, suf_scores, -jnp.inf)
            new_scores = jnp.where(new_usable, new_scores, -jnp.inf)
            suf_max = jnp.maximum(suf_scores.max(-1), new_scores.max(-1))
            suf_exps = jnp.exp(suf_scores - suf_max[..., None])
            new_exps = jnp.exp(new_scores - suf_max[..., None])
            suf_total = suf_exps.sum(-1) + new_exps.sum(-1)
            suf_w = lax.optimization_barrier(suf_exps.astype(jnp.bfloat16)).astype(jnp.float32)
            new_w = lax.optimization_barrier(new_exps.astype(jnp.bfloat16)).astype(jnp.float32)
            suf_sum = jnp.einsum('rqk,rkd->rqd', suf_w, own_values, precision=running_highest)
            suf_sum = suf_sum + jnp.einsum('rqk,kd->rqd', new_w, row_values, precision=running_highest)
            top = jnp.maximum(part_lse.max(-1), suf_max)
            part_w = jnp.exp(part_lse - top[..., None])
            own_w = jnp.exp(suf_max - top)
            totals = part_w.sum(-1) + own_w * suf_total
            summed = jnp.einsum('rqb,rqbd->rqd', part_w, part_out, precision=running_highest) + own_w[..., None] * suf_sum
            return (summed / totals[..., None]).reshape(block_rows, QPG * HD).astype(jnp.bfloat16)
        blocks = lax.map(one_block, jnp.arange(block_count, dtype=jnp.int32))
        return blocks.reshape(ROWS, QPG * HD)
    grouped = lax.map(head_group, jnp.arange(KVH, dtype=jnp.int32))
    attended = jnp.transpose(grouped, (1, 0, 2)).reshape(ROWS, HEADS * HD)
    return jnp.dot(attended, out_weight, preferred_element_type=jnp.float32).astype(jnp.bfloat16)
```

```python
import functools
import math

import jax
import jax.numpy as jnp
from jax import lax
from jax.experimental import pallas as pl
from jax.experimental.pallas import tpu as pltpu
from jax.sharding import PartitionSpec as P

HD = 128
QPG = 8
NY = 4
MESH = pl.DeviceIdType.MESH
SCALE2 = math.log2(math.e) / math.sqrt(HD)
LOG2E = math.log2(math.e)
LOW = -1e30
F32 = jnp.float32
BF16 = jnp.bfloat16


class Ring:
    def __init__(self, n, left, right, send_sem, recv_sem):
        self.n, self.left, self.right = n, left, right
        self.send_sem, self.recv_sem = send_sem, recv_sem
        self.last = n // 2

    def copy(self, way, k, src, dst):
        return pltpu.make_async_remote_copy(
            src_ref=src,
            dst_ref=dst,
            send_sem=self.send_sem.at[way, k - 1],
            recv_sem=self.recv_sem.at[way, k - 1],
            device_id=self.right if way == 0 else self.left,
            device_id_type=MESH,
        )


def kernel(
    nz,
    q_ref,
    pk_ref,
    pv_ref,
    nk_ref,
    nv_ref,
    ck_ref,
    cv_ref,
    rr_ref,
    cl_ref,
    w_ref,
    out_ref,
    kbuf,
    vbuf,
    qbuf,
    wbuf,
    ckb,
    cvb,
    nkb,
    nvb,
    acc,
    mst,
    osend,
    orecv,
    lsend,
    lrecv,
    att,
    psend,
    precv,
    fsend,
    frecv,
    loc_sem,
    qs,
    qr,
    ks,
    kr,
    ws,
    wr,
    os_,
    or_,
    ls,
    lr,
    as_,
    ar,
    ps,
    pr,
    fs,
    fr,
):
    nt = nz
    rows = q_ref.shape[0]
    keys = pk_ref.shape[0]
    reqs, slots = ck_ref.shape[0], ck_ref.shape[1]
    s_idx = lax.axis_index("seq")
    t = lax.axis_index("tp")
    z = s_idx // NY
    y = s_idx % NY

    def at_z(v):
        return (lax.rem(v + 2 * nz, nz) * NY + y, t)

    def at_y(v):
        return (z * NY + lax.rem(v + 2 * NY, NY), t)

    def at_t(v):
        return (s_idx, lax.rem(v + 2 * nt, nt))

    barrier = pltpu.get_barrier_semaphore()
    for i in range(1, nz):
        pl.semaphore_signal(barrier, inc=1, device_id=at_z(z + i), device_id_type=MESH)
    for i in range(1, NY):
        pl.semaphore_signal(barrier, inc=1, device_id=at_y(y + i), device_id_type=MESH)
    for i in range(1, nt):
        pl.semaphore_signal(barrier, inc=1, device_id=at_t(t + i), device_id_type=MESH)

    local = [
        pltpu.make_async_copy(q_ref, qbuf.at[0], loc_sem.at[0]),
        pltpu.make_async_copy(ck_ref, ckb, loc_sem.at[1]),
        pltpu.make_async_copy(cv_ref, cvb, loc_sem.at[2]),
        pltpu.make_async_copy(nk_ref, nkb.at[pl.ds(0, rows)], loc_sem.at[3]),
        pltpu.make_async_copy(nv_ref, nvb.at[pl.ds(0, rows)], loc_sem.at[4]),
        pltpu.make_async_copy(pk_ref, kbuf.at[0], loc_sem.at[5]),
        pltpu.make_async_copy(pv_ref, vbuf.at[0], loc_sem.at[6]),
        pltpu.make_async_copy(w_ref, wbuf.at[y], loc_sem.at[7]),
    ]
    for c in local:
        c.start()
    pl.semaphore_wait(barrier, nz + NY + nt - 3)

    half = rows // 2
    zl, zr = at_z(z - 1), at_z(z + 1)
    yl, yr = at_y(y - 1), at_y(y + 1)
    qring = Ring(nz, zl, zr, qs, qr)
    last = nz // 2
    halves = (pl.ds(0, half), pl.ds(half, half))

    def q_slot(way, k):
        return 2 * k - 1 if (way == 0 or k == last) else 2 * k

    def q_copy(way, k):
        dst = qbuf.at[q_slot(way, k)]
        if k == 1:
            src = q_ref
        else:
            src = qbuf.at[q_slot(way, k - 1)]
        if k == last:
            src, dst = src.at[halves[way]], dst.at[halves[way]]
        return qring.copy(way, k, src, dst)

    for way in range(2):
        q_copy(way, 1).start()

    def remote(src, dst, ssem, rsem, dev):
        return pltpu.make_async_remote_copy(
            src_ref=src,
            dst_ref=dst,
            send_sem=ssem,
            recv_sem=rsem,
            device_id=dev,
            device_id_type=MESH,
        )

    k_right = remote(pk_ref, kbuf.at[1], ks.at[0], kr.at[0], yr)
    v_right = remote(pv_ref, vbuf.at[1], ks.at[1], kr.at[1], yr)
    k_left = remote(pk_ref, kbuf.at[2], ks.at[2], kr.at[2], yl)
    v_left = remote(pv_ref, vbuf.at[2], ks.at[3], kr.at[3], yl)
    k_fwd = remote(kbuf.at[1], kbuf.at[3], ks.at[4], kr.at[4], yr)
    v_fwd = remote(vbuf.at[2], vbuf.at[3], ks.at[5], kr.at[5], yl)
    k_right.start()
    k_left.start()
    v_right.start()
    v_left.start()

    pad = nkb.shape[0]
    nkb[pl.ds(rows, pad - rows), :] = jnp.zeros((pad - rows, HD), BF16)
    nvb[pl.ds(rows, pad - rows), :] = jnp.zeros((pad - rows, HD), BF16)
    for c in local[:5]:
        c.wait()
    rr_lane = rr_ref[...]
    sub = lax.broadcasted_iota(jnp.int32, (rows, pad), 0)
    lane = lax.broadcasted_iota(jnp.int32, (rows, pad), 1)
    rr_all = jnp.broadcast_to(rr_lane, (rows, pad))
    rr_col = jnp.sum(jnp.where(sub == lane, rr_all, 0), axis=1, keepdims=True) - s_idx * reqs

    def queries_of(i):
        return jnp.concatenate(
            [qbuf[i, :, h * HD : (h + 1) * HD] for h in range(QPG)], axis=0
        )

    def scores(q, k):
        return lax.dot_general(q, k, (((1,), (1,)), ((), ())), preferred_element_type=F32)

    q_own = queries_of(0)
    parts = []
    slot_lane = lax.broadcasted_iota(jnp.int32, (rows, slots), 1)
    for j in range(reqs):
        ok = (rr_col == j) & (slot_lane < cl_ref[j])
        bias = jnp.where(ok, 0.0, LOW).astype(F32)
        parts.append(scores(q_own, ckb[j]) + jnp.concatenate([bias] * QPG, axis=0))
    ok = (rr_all - s_idx * reqs == rr_col) & (lane <= sub)
    bias = jnp.where(ok, 0.0, LOW).astype(F32)
    parts.append(scores(q_own, nkb[...]) + jnp.concatenate([bias] * QPG, axis=0))
    top = functools.reduce(jnp.maximum, [p.max(axis=1, keepdims=True) for p in parts])
    total = jnp.zeros((rows * QPG, 2 * HD), F32)
    for j, p in enumerate(parts):
        w = jnp.exp2((p - top) * SCALE2).astype(BF16)
        v = cvb[j] if j < reqs else nvb[...]
        vv = jnp.concatenate([v, jnp.ones_like(v)], axis=1)
        total = total + jnp.dot(w, vv, preferred_element_type=F32)
    acc[0] = total
    mst[0] = jnp.broadcast_to(top, (rows * QPG, HD))
    for i in range(1, nz):
        acc[i] = jnp.zeros((rows * QPG, 2 * HD), F32)
        mst[i] = jnp.full((rows * QPG, HD), LOW, F32)

    def flash(i, blk):
        q = queries_of(i)
        s = scores(q, kbuf[blk])
        chunks = [s[:, c * HD : (c + 1) * HD] for c in range(keys // HD)]
        m_old = mst[i]
        m_new = jnp.maximum(
            m_old, functools.reduce(jnp.maximum, chunks).max(axis=1, keepdims=True)
        )
        m2 = m_new * SCALE2
        w = jnp.concatenate(
            [jnp.exp2(c * SCALE2 - m2).astype(BF16) for c in chunks], axis=1
        )
        v = vbuf[blk]
        o = jnp.dot(w, jnp.concatenate([v, jnp.ones_like(v)], axis=1), preferred_element_type=F32)
        alpha = jnp.exp2(m_old * SCALE2 - m2)
        acc[i] = acc[i] * jnp.concatenate([alpha, alpha], axis=1) + o
        mst[i] = m_new

    for c in local[5:7]:
        c.wait()

    def first(p, carry):
        for k in range(1, last + 1):

            @pl.when(p == k - 1)
            def _(k=k):
                for way in range(2):
                    q_copy(way, k).wait_recv()
                    if k < last:
                        q_copy(way, k + 1).start()

        flash(2 * p, 0)
        flash(2 * p + 1, 0)
        return carry

    lax.fori_loop(0, last, first, 0)

    k_right.wait_recv()
    k_fwd.start()
    v_left.wait_recv()
    v_fwd.start()
    v_right.wait_recv()
    k_left.wait_recv()

    def middle(n, carry):
        p = lax.rem(n, last)
        blk = 1 + n // last
        flash(2 * p, blk)
        flash(2 * p + 1, blk)
        return carry

    lax.fori_loop(0, 2 * last, middle, 0)
    k_fwd.wait_recv()
    v_fwd.wait_recv()

    depth = w_ref.shape[0]
    whalf = (pl.ds(0, depth // 2), pl.ds(depth // 2, depth // 2))
    left_y = lax.rem(y + NY - 1, NY)
    right_y = lax.rem(y + 1, NY)
    w_right = remote(w_ref, wbuf.at[y], ws.at[0], wr.at[0], yr)
    w_left = remote(w_ref, wbuf.at[y], ws.at[1], wr.at[1], yl)
    w_fwd0 = remote(
        wbuf.at[left_y, whalf[0]], wbuf.at[left_y, whalf[0]], ws.at[2], wr.at[2], yr
    )
    w_fwd1 = remote(
        wbuf.at[right_y, whalf[1]], wbuf.at[right_y, whalf[1]], ws.at[3], wr.at[3], yl
    )
    w_right.start()
    w_left.start()

    lane8 = lax.broadcasted_iota(jnp.int32, (8, HD), 1)
    groups = rows // 8

    def o_copies(i):
        up = lax.rem(i, 2)
        off = ((i + 1) // 2) * (2 * up - 1)
        dev = at_z(z - off)
        return (
            remote(osend.at[i], orecv.at[i], os_.at[i], or_.at[i], dev),
            remote(lsend.at[i], lrecv.at[i], ls.at[i], lr.at[i], dev),
        )

    def finish(i):
        a = acc[i]
        l = a[:, HD:]
        osend[i] = (a[:, :HD] / l).astype(BF16)
        lse = mst[i] * SCALE2 + jnp.log(l) * LOG2E
        packed = jnp.zeros((8, HD), F32)
        for h in range(QPG):
            for g in range(groups):
                r0 = h * rows + g * 8
                packed = jnp.where(lane8 == g * 8 + h, lse[r0 : r0 + 8, :], packed)
        lsend[i] = packed

    def final(n, carry):
        p = last - 1 - n
        flash(2 * p, 3)
        flash(2 * p + 1, 3)
        finish(2 * p)
        finish(2 * p + 1)
        for c in o_copies(2 * p + 1):
            c.start()

        @pl.when(p > 0)
        def _():
            for c in o_copies(2 * p):
                c.start()

        return carry

    lax.fori_loop(0, last, final, 0)

    w_right.wait_recv()
    w_fwd0.start()
    w_left.wait_recv()
    w_fwd1.start()

    for i in range(nz - 1, 0, -1):
        for c in o_copies(i):
            c.wait_recv()

    lses = [lsend[0]] + [lrecv[i] for i in range(1, nz)]
    best = functools.reduce(jnp.maximum, lses)
    wts = [jnp.exp2(v - best) for v in lses]
    norm = functools.reduce(jnp.add, wts)
    wts = [v / norm for v in wts]
    for h in range(QPG):
        tot = jnp.zeros((rows, HD), F32)
        for i in range(nz):
            o = (osend if i == 0 else orecv)[i, h * rows : (h + 1) * rows, :].astype(F32)
            col = jnp.concatenate(
                [wts[i][:, g * 8 + h : g * 8 + h + 1] for g in range(groups)], axis=0
            )
            tot = tot + o * col
        att[z, :, h * HD : (h + 1) * HD] = tot.astype(BF16)

    aring = Ring(nz, zl, zr, as_, ar)

    def a_copy(way, k):
        origin = lax.rem(z + (1 - k if way == 0 else k - 1) + nz, nz)
        ref = att.at[origin]
        if k == last:
            ref = ref.at[halves[way]]
        return aring.copy(way, k, ref, ref)

    for way in range(2):
        a_copy(way, 1).start()
    for k in range(1, last + 1):
        for way in range(2):
            a_copy(way, k).wait_recv()
            if k < last:
                a_copy(way, k + 1).start()

    local[7].wait()
    w_fwd0.wait_recv()
    w_fwd1.wait_recv()
    cols = w_ref.shape[1]
    a_all = att[...].reshape(nz * rows, depth)
    for j in range(NY):
        pj = jnp.dot(a_all, wbuf[j], preferred_element_type=F32).astype(BF16)
        psend[:, :, j * cols : (j + 1) * cols] = pj.reshape(nz, rows, cols)

    def p_copy(e):
        dst_t = lax.rem(t + e, nt)
        return remote(psend.at[dst_t], precv.at[e], ps.at[e], pr.at[e], at_t(t + e))

    for e in range(1, nt):
        p_copy(e).start()
    tot = psend[t].astype(F32)
    for e in range(1, nt):
        p_copy(e).wait_recv()
        tot = tot + precv[e].astype(F32)
    tot = tot.astype(BF16)
    for j in range(NY):
        fsend[j] = tot[:, j * cols : (j + 1) * cols]

    def f_copy(e):
        dst_y = lax.rem(y + e, NY)
        return remote(fsend.at[dst_y], frecv.at[y], fs.at[e], fr.at[e], at_y(y + e))

    for e in range(1, NY):
        f_copy(e).start()
    frecv[y] = fsend[y]
    for e in range(1, NY):
        f_copy(e).wait_recv()
    out_ref[...] = frecv[...].reshape(NY * rows, cols)

    for way in range(2):
        for k in range(1, last + 1):
            q_copy(way, k).wait_send()
            a_copy(way, k).wait_send()
    for c in (k_right, v_right, k_left, v_left, k_fwd, v_fwd, w_right, w_left, w_fwd0, w_fwd1):
        c.wait_send()
    for i in range(1, nz):
        for c in o_copies(i):
            c.wait_send()
    for e in range(1, nt):
        p_copy(e).wait_send()
    for e in range(1, NY):
        f_copy(e).wait_send()


def body(nz, q, pk, pv, nk, nv, ck, cv, rr, cl, w):
    rows = q.shape[0]
    feat = q.shape[1]
    keys = pk.shape[0]
    reqs, slots = ck.shape[0], ck.shape[1]
    depth, cols = w.shape
    m = rows * QPG
    wide = NY * cols
    last = nz // 2
    vm = pltpu.VMEM
    dma = pltpu.SemaphoreType.DMA
    any_spec = pl.BlockSpec(memory_space=pl.ANY)
    vmem_spec = pl.BlockSpec(memory_space=pltpu.VMEM)
    smem_spec = pl.BlockSpec(memory_space=pltpu.SMEM)
    rr = jnp.pad(rr.reshape(1, rows), ((0, 0), (0, HD - rows)), constant_values=-1)
    return pl.pallas_call(
        functools.partial(kernel, nz),
        out_shape=jax.ShapeDtypeStruct((NY * rows, cols), BF16),
        in_specs=[any_spec] * 7 + [vmem_spec, smem_spec, any_spec],
        out_specs=vmem_spec,
        scratch_shapes=[
            vm((NY, keys, HD), BF16),
            vm((NY, keys, HD), BF16),
            vm((nz, rows, feat), BF16),
            vm((NY, depth, cols), BF16),
            vm((reqs, slots, HD), BF16),
            vm((reqs, slots, HD), BF16),
            vm((HD, HD), BF16),
            vm((HD, HD), BF16),
            vm((nz, m, 2 * HD), F32),
            vm((nz, m, HD), F32),
            vm((nz, m, HD), BF16),
            vm((nz, m, HD), BF16),
            vm((nz, 8, HD), F32),
            vm((nz, 8, HD), F32),
            vm((nz, rows, depth), BF16),
            vm((nz, rows, wide), BF16),
            vm((nz, rows, wide), BF16),
            vm((NY, rows, cols), BF16),
            vm((NY, rows, cols), BF16),
            dma((8,)),
            dma((2, last)),
            dma((2, last)),
            dma((6,)),
            dma((6,)),
            dma((4,)),
            dma((4,)),
            dma((nz,)),
            dma((nz,)),
            dma((nz,)),
            dma((nz,)),
            dma((2, last)),
            dma((2, last)),
            dma((nz,)),
            dma((nz,)),
            dma((NY,)),
            dma((NY,)),
        ],
        compiler_params=pltpu.CompilerParams(
            collective_id=0, has_side_effects=True, vmem_limit_bytes=48 * 1024 * 1024
        ),
    )(q, pk, pv, nk, nv, ck, cv, rr, cl, w)


def solution(mesh):
    nz = mesh.shape["seq"] // NY
    in_specs = (
        P("seq", "tp"),
        P("seq", "tp"),
        P("seq", "tp"),
        P("seq", "tp"),
        P("seq", "tp"),
        P("seq", None, "tp"),
        P("seq", None, "tp"),
        P("seq"),
        P("seq"),
        P("tp", "seq"),
    )
    return jax.shard_map(
        functools.partial(body, nz),
        mesh=mesh,
        in_specs=in_specs,
        out_specs=P("tp", "seq"),
        check_vma=False,
    )
```

```python
import functools
import math

import jax
import jax.numpy as jnp
from jax import lax
from jax.experimental import pallas as pl
from jax.experimental.pallas import tpu as pltpu
from jax.sharding import PartitionSpec as P

HD = 128
QPG = 8
NY = 4
MESH = pl.DeviceIdType.MESH
SCALE2 = math.log2(math.e) / math.sqrt(HD)
LOG2E = math.log2(math.e)
LOW = -1e30
F32 = jnp.float32
BF16 = jnp.bfloat16


def kernel(
    nz,
    q_ref,
    pk_ref,
    pv_ref,
    nk_ref,
    nv_ref,
    ck_ref,
    cv_ref,
    rr_ref,
    cl_ref,
    w_ref,
    out_ref,
    kbuf,
    vbuf,
    qbuf,
    wbuf,
    ckb,
    cvb,
    nkb,
    nvb,
    rrs,
    cls,
    sca,
    scb,
    acc,
    mst,
    osend,
    orecv,
    att,
    proj,
    psend,
    precv,
    fsend,
    frecv,
    loc_sem,
    qs,
    qr,
    ks,
    kr,
    ws,
    wr,
    os_,
    or_,
    as_,
    ar,
    ps,
    pr,
    fs,
    fr,
):
    nt = nz
    rows = q_ref.shape[0]
    keys = pk_ref.shape[0]
    reqs, slots = ck_ref.shape[0], ck_ref.shape[1]
    depth, cols = w_ref.shape
    last = nz // 2
    s_idx = lax.axis_index("seq")
    t = lax.axis_index("tp")
    z = s_idx // NY
    y = s_idx % NY

    def at_z(v):
        return (lax.rem(v + 2 * nz, nz) * NY + y, t)

    def at_y(v):
        return (z * NY + lax.rem(v + 2 * NY, NY), t)

    def at_t(v):
        return (s_idx, lax.rem(v + 2 * nt, nt))

    def remote(src, dst, ssem, rsem, dev):
        return pltpu.make_async_remote_copy(
            src_ref=src,
            dst_ref=dst,
            send_sem=ssem,
            recv_sem=rsem,
            device_id=dev,
            device_id_type=MESH,
        )

    def greet(dev):
        pl.semaphore_signal(barrier, inc=1, device_id=dev, device_id_type=MESH)

    barrier = pltpu.get_barrier_semaphore()
    greet(at_y(y + 1))
    greet(at_y(y - 1))
    greet(at_z(z + 1))
    greet(at_z(z - 1))
    for i in range(1, nt):
        greet(at_t(t + i))

    local = [
        pltpu.make_async_copy(q_ref, qbuf.at[0], loc_sem.at[0]),
        pltpu.make_async_copy(ck_ref, ckb, loc_sem.at[1]),
        pltpu.make_async_copy(cv_ref, cvb, loc_sem.at[2]),
        pltpu.make_async_copy(nk_ref, nkb.at[pl.ds(0, rows)], loc_sem.at[3]),
        pltpu.make_async_copy(nv_ref, nvb.at[pl.ds(0, rows)], loc_sem.at[4]),
        pltpu.make_async_copy(rr_ref, rrs, loc_sem.at[5]),
        pltpu.make_async_copy(cl_ref, cls, loc_sem.at[6]),
        pltpu.make_async_copy(pk_ref, kbuf.at[0], loc_sem.at[7]),
        pltpu.make_async_copy(pv_ref, vbuf.at[0], loc_sem.at[8]),
        pltpu.make_async_copy(w_ref, wbuf.at[y], loc_sem.at[9]),
    ]
    for c in local:
        c.start()
    pl.semaphore_wait(barrier, nt + 3)

    lo, hi = pl.ds(0, keys // 2), pl.ds(keys // 2, keys // 2)
    ways = (at_y(y + 1), at_y(y - 1))
    place = (lo, hi)

    def kv_copy(stage, way, which):
        buf = (kbuf, vbuf)[which]
        whole = (pk_ref, pv_ref)[which]
        sem = (stage - 1) * 4 + way * 2 + which
        if stage == 1:
            src = whole.at[place[way]]
        elif stage == 2:
            src = whole.at[place[1 - way]]
        else:
            src = buf.at[1, place[way]]
        return remote(src, buf.at[stage, place[way]], ks.at[sem], kr.at[sem], ways[way])

    def kv_stage(stage, act):
        for which in range(2):
            for way in range(2):
                act(kv_copy(stage, way, which))

    kv_stage(1, lambda c: c.start())

    half = rows // 2
    halves = (pl.ds(0, half), pl.ds(half, half))
    zways = (at_z(z + 1), at_z(z - 1))

    def q_slot(way, k):
        return 2 * k - 1 if (way == 0 or k == last) else 2 * k

    def q_copy(way, k):
        dst = qbuf.at[q_slot(way, k)]
        src = q_ref if k == 1 else qbuf.at[q_slot(way, k - 1)]
        if k == last:
            src, dst = src.at[halves[way]], dst.at[halves[way]]
        return remote(src, dst, qs.at[way, k - 1], qr.at[way, k - 1], zways[way])

    for way in range(2):
        q_copy(way, 1).start()

    pad = nkb.shape[0]
    nkb[pl.ds(rows, pad - rows), :] = jnp.zeros((pad - rows, HD), BF16)
    nvb[pl.ds(rows, pad - rows), :] = jnp.zeros((pad - rows, HD), BF16)
    for c in local[:7]:
        c.wait()
    sub = lax.broadcasted_iota(jnp.int32, (rows, pad), 0)
    lane = lax.broadcasted_iota(jnp.int32, (rows, pad), 1)
    rr_col = jnp.zeros((rows, pad), jnp.int32)
    rr_row = jnp.zeros((rows, pad), jnp.int32)
    for r in range(rows):
        req = rrs[r] - s_idx * reqs
        rr_col = jnp.where(sub == r, req, rr_col)
        rr_row = jnp.where(lane == r, req, rr_row)

    def queries_of(i, first=0, heads=QPG):
        return jnp.concatenate(
            [qbuf[i, :, h * HD : (h + 1) * HD] for h in range(first, first + heads)], axis=0
        )

    def scores(q, k):
        return lax.dot_general(q, k, (((1,), (1,)), ((), ())), preferred_element_type=F32)

    def with_ones(v):
        return jnp.concatenate([v, jnp.ones_like(v)], axis=1)

    q_own = queries_of(0)
    parts = []
    for j in range(reqs):
        biases = [
            jnp.where((rr_col == j) & (lane + c * pad < cls[j]), 0.0, LOW).astype(F32)
            for c in range(slots // pad)
        ]
        bias = jnp.concatenate(biases, axis=1)
        parts.append(scores(q_own, ckb[j]) + jnp.concatenate([bias] * QPG, axis=0))
    bias = jnp.where((rr_row == rr_col) & (lane <= sub), 0.0, LOW).astype(F32)
    parts.append(scores(q_own, nkb[...]) + jnp.concatenate([bias] * QPG, axis=0))
    top = functools.reduce(jnp.maximum, [p.max(axis=1, keepdims=True) for p in parts])
    total = jnp.zeros((rows * QPG, 2 * HD), F32)
    for j, p in enumerate(parts):
        w = jnp.exp2((p - top) * SCALE2).astype(BF16)
        v = cvb[j] if j < reqs else nvb[...]
        total = total + jnp.dot(w, with_ones(v), preferred_element_type=F32)
    acc[0] = total
    mst[0] = jnp.broadcast_to(top, (rows * QPG, HD))
    for i in range(1, nz):
        acc[i] = jnp.zeros((rows * QPG, 2 * HD), F32)
        mst[i] = jnp.full((rows * QPG, HD), LOW, F32)

    kv_stage(2, lambda c: c.start())

    def fill(buf, blk, picks):
        q = jnp.concatenate([queries_of(i, f, n) for i, f, n in picks], axis=0)
        buf[...] = scores(q, kbuf[blk])

    def absorb(buf, blk, picks):
        ws_, alphas = [], []
        at = 0
        for i, f, n in picks:
            m = n * rows
            own = pl.ds(f * rows, m)
            chunks = [buf[at : at + m, c * HD : (c + 1) * HD] for c in range(keys // HD)]
            at += m
            m_old = mst[i, own]
            m_new = jnp.maximum(
                m_old, functools.reduce(jnp.maximum, chunks).max(axis=1, keepdims=True)
            )
            m2 = m_new * SCALE2
            ws_.append(
                jnp.concatenate([jnp.exp2(c * SCALE2 - m2).astype(BF16) for c in chunks], axis=1)
            )
            alphas.append(jnp.exp2(m_old * SCALE2 - m2))
            mst[i, own] = m_new
        o = jnp.dot(
            jnp.concatenate(ws_, axis=0), with_ones(vbuf[blk]), preferred_element_type=F32
        )
        at = 0
        for (i, f, n), alpha in zip(picks, alphas):
            m = n * rows
            own = pl.ds(f * rows, m)
            acc[i, own] = acc[i, own] * jnp.concatenate([alpha, alpha], axis=1) + o[at : at + m]
            at += m

    late = max(last - 2, 0)
    early = list(range(late))
    order = [(0, p) for p in early[:2]] + [(1, p) for p in early[:2]]
    for p in early[2:]:
        order += [(0, p), (1, p)]
    tail = list(range(late, last))
    if tail:
        order += [(0, tail[0]), (1, tail[0])]
    order += [(2, p) for p in early + tail[:1]]
    for p in tail[1:]:
        order += [(0, p), (1, p), (2, p)]
    need_q = {}
    for n, (b, p) in enumerate(order):
        need_q.setdefault(p, n)
    need_b = {b: min(n for n, o in enumerate(order) if o[0] == b) for b in (0, 1, 2)}

    def waits(n):
        def when(cond, act):
            if isinstance(n, int):
                if n == cond:
                    act()
            else:
                pl.when(n == cond)(act)

        def q_step(k):
            for way in range(2):
                q_copy(way, k).wait_recv()
                if k < last:
                    q_copy(way, k + 1).start()

        def own():
            for c in local[7:9]:
                c.wait()

        def blk1():
            kv_stage(1, lambda c: c.wait_recv())
            kv_stage(3, lambda c: c.start())

        when(need_b[0], own)
        for p in range(last):
            when(need_q[p], lambda p=p: q_step(p + 1))
        when(need_b[1], blk1)
        when(need_b[2], lambda: kv_stage(2, lambda c: c.wait_recv()))

    def tile(n):
        if isinstance(n, int):
            b, p = order[n]
        else:
            b = p = 0
            for m, (bb, pp) in enumerate(order):
                b = jnp.where(n == m, bb, b)
                p = jnp.where(n == m, pp, p)
        return b, [(2 * p, 0, QPG), (2 * p + 1, 0, QPG)]

    count = len(order)
    waits(0)
    fill(sca, *tile(0))

    def step(m, carry):
        for buf, other, n in ((sca, scb, 2 * m), (scb, sca, 2 * m + 1)):
            waits(n + 1)
            fill(other, *tile(n + 1))
            absorb(buf, *tile(n))
        return carry

    pairs = (count - 1) // 2
    lax.fori_loop(0, pairs, step, 0)
    rest = list(range(2 * pairs, count))
    bufs = (sca, scb)
    for n in rest:
        if n + 1 < count:
            waits(n + 1)
            fill(bufs[(n + 1) % 2], *tile(n + 1))
        absorb(bufs[n % 2], *tile(n))

    wlo, whi = pl.ds(0, depth // 2), pl.ds(depth // 2, depth // 2)
    wplace = (wlo, whi)
    origin = (lax.rem(y + NY - 1, NY), lax.rem(y + 1, NY))

    def w_copy(stage, way):
        sem = (stage - 1) * 2 + way
        if stage == 3:
            src = dst = wbuf.at[origin[way], wplace[way]]
        else:
            part = wplace[way] if stage == 1 else wplace[1 - way]
            src, dst = w_ref.at[part], wbuf.at[y, part]
        return remote(src, dst, ws.at[sem], wr.at[sem], ways[way])

    def w_stage(stage, act):
        for way in range(2):
            act(w_copy(stage, way))

    lane8 = lax.broadcasted_iota(jnp.int32, (8, HD), 1)
    groups = rows // 8
    hh = QPG // 2
    mh = hh * rows
    nslot = max(nz // 2, 1)

    def o_copy(c, i):
        if i % 2:
            dev = at_z(z - (i + 1) // 2)
        else:
            dev = at_z(z + i // 2)
        return remote(osend.at[c, i], orecv.at[c, i], os_.at[c, i], or_.at[c, i], dev)

    def finish(c, i):
        own = pl.ds(c * mh, mh)
        a = acc[i, own]
        l = a[:, HD:]
        osend[c, i, :mh] = (a[:, :HD] / l).astype(BF16)
        lse = mst[i, own] * SCALE2 + jnp.log(l) * LOG2E
        packed = jnp.zeros((8, HD), F32)
        for h in range(hh):
            for g in range(groups):
                r0 = h * rows + g * 8
                packed = jnp.where(lane8 == g * 8 + h, lse[r0 : r0 + 8, :], packed)
        p1 = packed.astype(BF16).astype(F32)
        p2 = (packed - p1).astype(BF16).astype(F32)
        p3 = (packed - p1 - p2).astype(BF16).astype(F32)
        p13 = p1 + pltpu.roll(p3, 32, 1)
        osend[c, i, mh:] = jnp.concatenate([p13, p2], axis=0).astype(BF16)

    finals = []
    for c in range(2):
        for g in range(nz // nslot - 1, -1, -1):
            finals.append((c, [(i, c * hh, hh) for i in range(g * nslot + nslot - 1, g * nslot - 1, -1)]))
    frows = nslot * mh
    fbufs = (sca.at[pl.ds(0, frows)], scb.at[pl.ds(0, frows)])

    kv_stage(3, lambda c: c.wait_recv())
    w_stage(1, lambda c: c.start())
    fill(fbufs[0], 3, finals[0][1])
    for n, (c, picks) in enumerate(finals):
        if n + 1 < len(finals):
            fill(fbufs[(n + 1) % 2], 3, finals[n + 1][1])
        absorb(fbufs[n % 2], 3, picks)
        for i, _, _ in picks:
            finish(c, i)
            if i > 0:
                o_copy(c, i).start()
        if n == 1:
            w_stage(2, lambda c: c.start())

    far_first = sorted(range(1, nz), key=lambda d: -min(d, nz - d))

    def a_copy(c, d):
        ref = att.at[c, z]
        return remote(ref, ref, as_.at[c, d], ar.at[c, d], at_z(z + d))

    def merge(c):
        for i in range(1, nz):
            o_copy(c, i).wait_recv()
        lses = []
        for i in range(nz):
            x = (osend if i == 0 else orecv)[c, i, mh:].astype(F32)
            lses.append(x[:8] + x[8:] + pltpu.roll(x[:8], HD - 32, 1))
        best = functools.reduce(jnp.maximum, lses)
        wts = [jnp.exp2(v - best) for v in lses]
        norm = functools.reduce(jnp.add, wts)
        wts = [v / norm for v in wts]
        for h in range(hh):
            tot = jnp.zeros((rows, HD), F32)
            for i in range(nz):
                o = (osend if i == 0 else orecv)[c, i, h * rows : (h + 1) * rows, :].astype(F32)
                col = jnp.concatenate(
                    [wts[i][:, g * 8 + h : g * 8 + h + 1] for g in range(groups)], axis=0
                )
                tot = tot + o * col
            att[c, z, :, h * HD : (h + 1) * HD] = tot.astype(BF16)
        for d in far_first:
            a_copy(c, d).start()

    merge(0)
    w_stage(1, lambda c: c.wait_recv())
    w_stage(3, lambda c: c.start())
    merge(1)

    local[9].wait()
    w_stage(2, lambda c: c.wait_recv())
    w_stage(3, lambda c: c.wait_recv())
    hd = depth // 2
    for c in range(2):
        for d in far_first:
            a_copy(c, d).wait_recv()
        a_all = att[c].reshape(nz * rows, hd)
        for j in range(NY):
            out = jnp.dot(a_all, wbuf[j, c * hd : (c + 1) * hd], preferred_element_type=F32)
            if c == 0:
                proj[:, j * cols : (j + 1) * cols] = out
            else:
                out = (out + proj[:, j * cols : (j + 1) * cols]).astype(BF16)
                psend[:, :, j * cols : (j + 1) * cols] = out.reshape(nz, rows, cols)

    def p_copy(e):
        dst_t = lax.rem(t + e, nt)
        return remote(psend.at[dst_t], precv.at[e], ps.at[e], pr.at[e], at_t(t + e))

    for e in range(1, nt):
        p_copy(e).start()
    tot = psend[t].astype(F32)
    for e in range(1, nt):
        p_copy(e).wait_recv()
        tot = tot + precv[e].astype(F32)
    tot = tot.astype(BF16)
    for j in range(NY):
        fsend[j] = tot[:, j * cols : (j + 1) * cols]

    def f_copy(e):
        dst_y = lax.rem(y + e, NY)
        return remote(fsend.at[dst_y], frecv.at[y], fs.at[e], fr.at[e], at_y(y + e))

    for e in range(1, NY):
        f_copy(e).start()
    frecv[y] = fsend[y]
    for e in range(1, NY):
        f_copy(e).wait_recv()
    out_ref[...] = frecv[...].reshape(NY * rows, cols)

    for way in range(2):
        for k in range(1, last + 1):
            q_copy(way, k).wait_send()
    for stage in (1, 2, 3):
        kv_stage(stage, lambda c: c.wait_send())
        w_stage(stage, lambda c: c.wait_send())
    for c in range(2):
        for i in range(1, nz):
            o_copy(c, i).wait_send()
            a_copy(c, i).wait_send()
    for e in range(1, nt):
        p_copy(e).wait_send()
    for e in range(1, NY):
        f_copy(e).wait_send()


def body(nz, q, pk, pv, nk, nv, ck, cv, rr, cl, w):
    rows = q.shape[0]
    feat = q.shape[1]
    keys = pk.shape[0]
    reqs, slots = ck.shape[0], ck.shape[1]
    depth, cols = w.shape
    m = rows * QPG
    wide = NY * cols
    last = nz // 2
    vm = pltpu.VMEM
    dma = pltpu.SemaphoreType.DMA
    any_spec = pl.BlockSpec(memory_space=pl.ANY)
    vmem_spec = pl.BlockSpec(memory_space=pltpu.VMEM)
    return pl.pallas_call(
        functools.partial(kernel, nz),
        out_shape=jax.ShapeDtypeStruct((NY * rows, cols), BF16),
        in_specs=[any_spec] * 10,
        out_specs=vmem_spec,
        scratch_shapes=[
            vm((NY, keys, HD), BF16),
            vm((NY, keys, HD), BF16),
            vm((nz, rows, feat), BF16),
            vm((NY, depth, cols), BF16),
            vm((reqs, slots, HD), BF16),
            vm((reqs, slots, HD), BF16),
            vm((HD, HD), BF16),
            vm((HD, HD), BF16),
            pltpu.SMEM((rows,), jnp.int32),
            pltpu.SMEM((reqs,), jnp.int32),
            vm((2 * m, keys), F32),
            vm((2 * m, keys), F32),
            vm((nz, m, 2 * HD), F32),
            vm((nz, m, HD), F32),
            vm((2, nz, m // 2 + 16, HD), BF16),
            vm((2, nz, m // 2 + 16, HD), BF16),
            vm((2, nz, rows, depth // 2), BF16),
            vm((nz * rows, wide), F32),
            vm((nz, rows, wide), BF16),
            vm((nz, rows, wide), BF16),
            vm((NY, rows, cols), BF16),
            vm((NY, rows, cols), BF16),
            dma((10,)),
            dma((2, last)),
            dma((2, last)),
            dma((12,)),
            dma((12,)),
            dma((6,)),
            dma((6,)),
            dma((2, nz)),
            dma((2, nz)),
            dma((2, nz)),
            dma((2, nz)),
            dma((nz,)),
            dma((nz,)),
            dma((NY,)),
            dma((NY,)),
        ],
        compiler_params=pltpu.CompilerParams(
            collective_id=0, has_side_effects=True, vmem_limit_bytes=60 * 1024 * 1024
        ),
    )(q, pk, pv, nk, nv, ck, cv, rr, cl, w)


def solution(mesh):
    nz = mesh.shape["seq"] // NY
    in_specs = (
        P("seq", "tp"),
        P("seq", "tp"),
        P("seq", "tp"),
        P("seq", "tp"),
        P("seq", "tp"),
        P("seq", None, "tp"),
        P("seq", None, "tp"),
        P("seq"),
        P("seq"),
        P("tp", "seq"),
    )
    return jax.shard_map(
        functools.partial(body, nz),
        mesh=mesh,
        in_specs=in_specs,
        out_specs=P("tp", "seq"),
        check_vma=False,
    )
```

```python
import functools
import math

import jax
import jax.numpy as jnp
from jax import lax
from jax.experimental import pallas as pl
from jax.experimental.pallas import tpu as pltpu
from jax.sharding import PartitionSpec as P

HD = 128
QPG = 8
NY = 4
MESH = pl.DeviceIdType.MESH
SCALE2 = math.log2(math.e) / math.sqrt(HD)
LOG2E = math.log2(math.e)
LOW = -1e30
F32 = jnp.float32
BF16 = jnp.bfloat16


def kernel(
    nz,
    q_ref,
    pk_ref,
    pv_ref,
    nk_ref,
    nv_ref,
    ck_ref,
    cv_ref,
    rr_ref,
    cl_ref,
    w_ref,
    out_ref,
    kbuf,
    vbuf,
    qbuf,
    wbuf,
    ckb,
    cvb,
    nkb,
    nvb,
    rrs,
    cls,
    sca,
    scb,
    acc,
    mst,
    osend,
    orecv,
    att,
    psend,
    precv,
    fsend,
    frecv,
    loc_sem,
    qs,
    qr,
    ks,
    kr,
    ws,
    wr,
    os_,
    or_,
    as_,
    ar,
    ps,
    pr,
    fs,
    fr,
):
    nt = nz
    rows = q_ref.shape[0]
    keys = pk_ref.shape[0]
    reqs, slots = ck_ref.shape[0], ck_ref.shape[1]
    depth, cols = w_ref.shape
    last = nz // 2
    s_idx = lax.axis_index("seq")
    t = lax.axis_index("tp")
    z = s_idx // NY
    y = s_idx % NY

    def at_z(v):
        return (lax.rem(v + 2 * nz, nz) * NY + y, t)

    def at_y(v):
        return (z * NY + lax.rem(v + 2 * NY, NY), t)

    def at_t(v):
        return (s_idx, lax.rem(v + 2 * nt, nt))

    def remote(src, dst, ssem, rsem, dev):
        return pltpu.make_async_remote_copy(
            src_ref=src,
            dst_ref=dst,
            send_sem=ssem,
            recv_sem=rsem,
            device_id=dev,
            device_id_type=MESH,
        )

    def greet(dev):
        pl.semaphore_signal(barrier, inc=1, device_id=dev, device_id_type=MESH)

    barrier = pltpu.get_barrier_semaphore()
    greet(at_y(y + 1))
    greet(at_y(y - 1))
    greet(at_z(z + 1))
    greet(at_z(z - 1))
    for i in range(1, nt):
        greet(at_t(t + i))

    local = [
        pltpu.make_async_copy(q_ref, qbuf.at[0], loc_sem.at[0]),
        pltpu.make_async_copy(ck_ref, ckb, loc_sem.at[1]),
        pltpu.make_async_copy(cv_ref, cvb, loc_sem.at[2]),
        pltpu.make_async_copy(nk_ref, nkb.at[pl.ds(0, rows)], loc_sem.at[3]),
        pltpu.make_async_copy(nv_ref, nvb.at[pl.ds(0, rows)], loc_sem.at[4]),
        pltpu.make_async_copy(rr_ref, rrs, loc_sem.at[5]),
        pltpu.make_async_copy(cl_ref, cls, loc_sem.at[6]),
        pltpu.make_async_copy(pk_ref, kbuf.at[0], loc_sem.at[7]),
        pltpu.make_async_copy(pv_ref, vbuf.at[0], loc_sem.at[8]),
        pltpu.make_async_copy(w_ref, wbuf.at[y], loc_sem.at[9]),
    ]
    pl.semaphore_wait(barrier, nt + 3)

    lo, hi = pl.ds(0, keys // 2), pl.ds(keys // 2, keys // 2)
    ways = (at_y(y + 1), at_y(y - 1))
    place = (lo, hi)

    def kv_copy(stage, way, which):
        buf = (kbuf, vbuf)[which]
        whole = (pk_ref, pv_ref)[which]
        sem = (stage - 1) * 4 + way * 2 + which
        if stage == 1:
            src = whole.at[place[way]]
        elif stage == 2:
            src = whole.at[place[1 - way]]
        else:
            src = buf.at[1, place[way]]
        return remote(src, buf.at[stage, place[way]], ks.at[sem], kr.at[sem], ways[way])

    def kv_stage(stage, act):
        for which in range(2):
            for way in range(2):
                act(kv_copy(stage, way, which))

    kv_stage(1, lambda c: c.start())

    half = rows // 2
    halves = (pl.ds(0, half), pl.ds(half, half))
    zways = (at_z(z + 1), at_z(z - 1))

    def q_slot(way, k):
        return 2 * k - 1 if (way == 0 or k == last) else 2 * k

    def q_copy(way, k):
        dst = qbuf.at[q_slot(way, k)]
        src = q_ref if k == 1 else qbuf.at[q_slot(way, k - 1)]
        if k == last:
            src, dst = src.at[halves[way]], dst.at[halves[way]]
        return remote(src, dst, qs.at[way, k - 1], qr.at[way, k - 1], zways[way])

    for way in range(2):
        q_copy(way, 1).start()
    for c in local:
        c.start()

    pad = nkb.shape[0]
    nkb[pl.ds(rows, pad - rows), :] = jnp.zeros((pad - rows, HD), BF16)
    nvb[pl.ds(rows, pad - rows), :] = jnp.zeros((pad - rows, HD), BF16)
    for c in local[:7]:
        c.wait()
    sub = lax.broadcasted_iota(jnp.int32, (rows, pad), 0)
    lane = lax.broadcasted_iota(jnp.int32, (rows, pad), 1)
    rr_col = jnp.zeros((rows, pad), jnp.int32)
    rr_row = jnp.zeros((rows, pad), jnp.int32)
    for r in range(rows):
        req = rrs[r] - s_idx * reqs
        rr_col = jnp.where(sub == r, req, rr_col)
        rr_row = jnp.where(lane == r, req, rr_row)

    def queries_of(i, first=0, parts=2):
        return jnp.concatenate(
            [
                qbuf[i, c * half : (c + 1) * half, h * HD : (h + 1) * HD]
                for c in range(first, first + parts)
                for h in range(QPG)
            ],
            axis=0,
        )

    def per_head(bias):
        return jnp.concatenate([bias[:half]] * QPG + [bias[half:]] * QPG, axis=0)

    def scores(q, k):
        return lax.dot_general(q, k, (((1,), (1,)), ((), ())), preferred_element_type=F32)

    def with_ones(v):
        return jnp.concatenate([v, jnp.ones_like(v)], axis=1)

    q_own = queries_of(0)
    parts = []
    for j in range(reqs):
        biases = [
            jnp.where((rr_col == j) & (lane + c * pad < cls[j]), 0.0, LOW).astype(F32)
            for c in range(slots // pad)
        ]
        bias = jnp.concatenate(biases, axis=1)
        parts.append(scores(q_own, ckb[j]) + per_head(bias))
    bias = jnp.where((rr_row == rr_col) & (lane <= sub), 0.0, LOW).astype(F32)
    parts.append(scores(q_own, nkb[...]) + per_head(bias))
    top = functools.reduce(jnp.maximum, [p.max(axis=1, keepdims=True) for p in parts])
    total = jnp.zeros((rows * QPG, 2 * HD), F32)
    for j, p in enumerate(parts):
        w = jnp.exp2((p - top) * SCALE2).astype(BF16)
        v = cvb[j] if j < reqs else nvb[...]
        total = total + jnp.dot(w, with_ones(v), preferred_element_type=F32)
    acc[0] = total
    mst[0] = jnp.broadcast_to(top, (rows * QPG, HD))
    for i in range(1, nz):
        acc[i] = jnp.zeros((rows * QPG, 2 * HD), F32)
        mst[i] = jnp.full((rows * QPG, HD), LOW, F32)

    mh = half * QPG

    def fill(buf, blk, picks):
        q = jnp.concatenate([queries_of(i, f, n) for i, f, n in picks], axis=0)
        buf[...] = scores(q, kbuf[blk])

    def absorb(buf, blk, picks):
        ws_, alphas = [], []
        at = 0
        for i, f, n in picks:
            m = n * mh
            own = pl.ds(f * mh, m)
            chunks = [buf[at : at + m, c * HD : (c + 1) * HD] for c in range(keys // HD)]
            at += m
            m_old = mst[i, own]
            m_new = jnp.maximum(
                m_old, functools.reduce(jnp.maximum, chunks).max(axis=1, keepdims=True)
            )
            m2 = m_new * SCALE2
            ws_.append(
                jnp.concatenate([jnp.exp2(c * SCALE2 - m2).astype(BF16) for c in chunks], axis=1)
            )
            alphas.append(jnp.exp2(m_old * SCALE2 - m2))
            mst[i, own] = m_new
        o = jnp.dot(
            jnp.concatenate(ws_, axis=0), with_ones(vbuf[blk]), preferred_element_type=F32
        )
        at = 0
        for (i, f, n), alpha in zip(picks, alphas):
            m = n * mh
            own = pl.ds(f * mh, m)
            acc[i, own] = acc[i, own] * jnp.concatenate([alpha, alpha], axis=1) + o[at : at + m]
            at += m

    late = max(last - 2, 0)
    early = list(range(late))
    order = [(0, p) for p in early[:2]] + [(1, p) for p in early[:2]]
    for p in early[2:]:
        order += [(0, p), (1, p)]
    tail = list(range(late, last))
    if tail:
        order += [(0, tail[0]), (1, tail[0])]
    order += [(2, p) for p in early + tail[:1]]
    for p in tail[1:]:
        order += [(0, p), (1, p), (2, p)]
    need_q = {}
    for n, (b, p) in enumerate(order):
        need_q.setdefault(p, n)
    need_b = {b: min(n for n, o in enumerate(order) if o[0] == b) for b in (0, 1, 2)}

    def waits(n):
        def when(cond, act):
            if isinstance(n, int):
                if n == cond:
                    act()
            else:
                pl.when(n == cond)(act)

        def q_step(k):
            for way in range(2):
                q_copy(way, k).wait_recv()
                if k < last:
                    q_copy(way, k + 1).start()

        def own():
            for c in local[7:9]:
                c.wait()

        def blk1():
            kv_stage(1, lambda c: c.wait_recv())
            kv_stage(3, lambda c: c.start())

        when(need_b[0], own)
        for p in range(last):
            when(need_q[p], lambda p=p: q_step(p + 1))
        when(need_b[1], blk1)
        when(need_b[2], lambda: kv_stage(2, lambda c: c.wait_recv()))

    def tile(n):
        if isinstance(n, int):
            b, p = order[n]
        else:
            b = p = 0
            for m, (bb, pp) in enumerate(order):
                b = jnp.where(n == m, bb, b)
                p = jnp.where(n == m, pp, p)
        return b, [(2 * p, 0, 2), (2 * p + 1, 0, 2)]

    count = len(order)
    waits(0)
    fill(sca, *tile(0))
    kv_stage(2, lambda c: c.start())

    def step(m, carry):
        for buf, other, n in ((sca, scb, 2 * m), (scb, sca, 2 * m + 1)):
            waits(n + 1)
            fill(other, *tile(n + 1))
            absorb(buf, *tile(n))
        return carry

    pairs = (count - 1) // 2
    lax.fori_loop(0, pairs, step, 0)
    rest = list(range(2 * pairs, count))
    bufs = (sca, scb)
    for n in rest:
        if n + 1 < count:
            waits(n + 1)
            fill(bufs[(n + 1) % 2], *tile(n + 1))
        absorb(bufs[n % 2], *tile(n))

    wlo, whi = pl.ds(0, depth // 2), pl.ds(depth // 2, depth // 2)
    wplace = (wlo, whi)
    origin = (lax.rem(y + NY - 1, NY), lax.rem(y + 1, NY))

    def w_copy(stage, way):
        sem = (stage - 1) * 2 + way
        if stage == 3:
            src = dst = wbuf.at[origin[way], wplace[way]]
        else:
            part = wplace[way] if stage == 1 else wplace[1 - way]
            src, dst = w_ref.at[part], wbuf.at[y, part]
        return remote(src, dst, ws.at[sem], wr.at[sem], ways[way])

    def w_stage(stage, act):
        for way in range(2):
            act(w_copy(stage, way))

    lane8 = lax.broadcasted_iota(jnp.int32, (8, HD), 1)
    groups = half // 8
    nslot = max(nz // 2, 1)

    def o_copy(c, i):
        if i % 2:
            dev = at_z(z - (i + 1) // 2)
        else:
            dev = at_z(z + i // 2)
        return remote(osend.at[c, i], orecv.at[c, i], os_.at[c, i], or_.at[c, i], dev)

    def finish(c, i):
        own = pl.ds(c * mh, mh)
        a = acc[i, own]
        l = a[:, HD:]
        osend[c, i, :mh] = (a[:, :HD] / l).astype(BF16)
        m = mst[i, own]
        top_of = jnp.zeros((8, HD), F32)
        sum_of = jnp.ones((8, HD), F32)
        for h in range(QPG):
            for g in range(groups):
                r0 = h * half + g * 8
                pick = lane8 == g * 8 + h
                top_of = jnp.where(pick, m[r0 : r0 + 8, :], top_of)
                sum_of = jnp.where(pick, l[r0 : r0 + 8, :], sum_of)
        packed = top_of * SCALE2 + jnp.log(sum_of) * LOG2E
        p1 = packed.astype(BF16).astype(F32)
        p2 = (packed - p1).astype(BF16).astype(F32)
        p3 = (packed - p1 - p2).astype(BF16).astype(F32)
        p13 = p1 + pltpu.roll(p3, 32, 1)
        osend[c, i, mh:] = jnp.concatenate([p13, p2], axis=0).astype(BF16)

    finals = []
    for c in range(2):
        for g in range(nz // nslot - 1, -1, -1):
            picks = range(g * nslot + nslot - 1, g * nslot - 1, -1)
            finals.append((c, [(i, c, 1) for i in picks]))
    frows = nslot * mh
    fbufs = (sca.at[pl.ds(0, frows)], scb.at[pl.ds(0, frows)])

    kv_stage(3, lambda c: c.wait_recv())
    w_stage(1, lambda c: c.start())
    fill(fbufs[0], 3, finals[0][1])
    for n, (c, picks) in enumerate(finals):
        if n + 1 < len(finals):
            fill(fbufs[(n + 1) % 2], 3, finals[n + 1][1])
        absorb(fbufs[n % 2], 3, picks)
        for i, _, _ in picks:
            finish(c, i)
            if i > 0:
                o_copy(c, i).start()
        if n == 1:
            w_stage(2, lambda c: c.start())

    far_first = sorted(range(1, nz), key=lambda d: -min(d, nz - d))

    def a_copy(c, d):
        ref = att.at[c, z]
        return remote(ref, ref, as_.at[c, d], ar.at[c, d], at_z(z + d))

    def merge(c):
        for i in range(1, nz):
            o_copy(c, i).wait_recv()
        lses = []
        for i in range(nz):
            x = (osend if i == 0 else orecv)[c, i, mh:].astype(F32)
            lses.append(x[:8] + x[8:] + pltpu.roll(x[:8], HD - 32, 1))
        best = functools.reduce(jnp.maximum, lses)
        wts = [jnp.exp2(v - best) for v in lses]
        norm = functools.reduce(jnp.add, wts)
        wts = [v / norm for v in wts]
        for h in range(QPG):
            tot = jnp.zeros((half, HD), F32)
            for i in range(nz):
                o = (osend if i == 0 else orecv)[c, i, h * half : (h + 1) * half, :].astype(F32)
                col = jnp.concatenate(
                    [wts[i][:, g * 8 + h : g * 8 + h + 1] for g in range(groups)], axis=0
                )
                tot = tot + o * col
            att[c, z, :, h * HD : (h + 1) * HD] = tot.astype(BF16)
        for d in far_first:
            a_copy(c, d).start()

    merge(0)
    w_stage(1, lambda c: c.wait_recv())
    w_stage(3, lambda c: c.start())
    merge(1)

    local[9].wait()
    w_stage(2, lambda c: c.wait_recv())
    w_stage(3, lambda c: c.wait_recv())

    def p_copy(c, e):
        dst_t = lax.rem(t + e, nt)
        return remote(psend.at[c, dst_t], precv.at[c, e], ps.at[c, e], pr.at[c, e], at_t(t + e))

    for c in range(2):
        for d in far_first:
            a_copy(c, d).wait_recv()
        a_all = att[c].reshape(nz * half, depth)
        for j in range(NY):
            out = jnp.dot(a_all, wbuf[j], preferred_element_type=F32).astype(BF16)
            psend[c, :, :, j * cols : (j + 1) * cols] = out.reshape(nz, half, cols)
        for e in range(1, nt):
            p_copy(c, e).start()

    def f_copy(c, e):
        dst_y = lax.rem(y + e, NY)
        return remote(fsend.at[c, dst_y], frecv.at[c, y], fs.at[c, e], fr.at[c, e], at_y(y + e))

    for c in range(2):
        tot = psend[c, t].astype(F32)
        for e in range(1, nt):
            p_copy(c, e).wait_recv()
            tot = tot + precv[c, e].astype(F32)
        tot = tot.astype(BF16)
        for j in range(NY):
            fsend[c, j] = tot[:, j * cols : (j + 1) * cols]
        for e in range(1, NY):
            f_copy(c, e).start()
        frecv[c, y] = fsend[c, y]
    for c in range(2):
        for e in range(1, NY):
            f_copy(c, e).wait_recv()
        for j in range(NY):
            out_ref[j * rows + c * half : j * rows + (c + 1) * half, :] = frecv[c, j]

    for way in range(2):
        for k in range(1, last + 1):
            q_copy(way, k).wait_send()
    for stage in (1, 2, 3):
        kv_stage(stage, lambda c: c.wait_send())
        w_stage(stage, lambda c: c.wait_send())
    for c in range(2):
        for i in range(1, nz):
            o_copy(c, i).wait_send()
            a_copy(c, i).wait_send()
        for e in range(1, nt):
            p_copy(c, e).wait_send()
        for e in range(1, NY):
            f_copy(c, e).wait_send()


def body(nz, q, pk, pv, nk, nv, ck, cv, rr, cl, w):
    rows = q.shape[0]
    feat = q.shape[1]
    keys = pk.shape[0]
    reqs, slots = ck.shape[0], ck.shape[1]
    depth, cols = w.shape
    m = rows * QPG
    wide = NY * cols
    last = nz // 2
    vm = pltpu.VMEM
    dma = pltpu.SemaphoreType.DMA
    any_spec = pl.BlockSpec(memory_space=pl.ANY)
    vmem_spec = pl.BlockSpec(memory_space=pltpu.VMEM)
    return pl.pallas_call(
        functools.partial(kernel, nz),
        out_shape=jax.ShapeDtypeStruct((NY * rows, cols), BF16),
        in_specs=[any_spec] * 10,
        out_specs=vmem_spec,
        scratch_shapes=[
            vm((NY, keys, HD), BF16),
            vm((NY, keys, HD), BF16),
            vm((nz, rows, feat), BF16),
            vm((NY, depth, cols), BF16),
            vm((reqs, slots, HD), BF16),
            vm((reqs, slots, HD), BF16),
            vm((HD, HD), BF16),
            vm((HD, HD), BF16),
            pltpu.SMEM((rows,), jnp.int32),
            pltpu.SMEM((reqs,), jnp.int32),
            vm((2 * m, keys), F32),
            vm((2 * m, keys), F32),
            vm((nz, m, 2 * HD), F32),
            vm((nz, m, HD), F32),
            vm((2, nz, m // 2 + 16, HD), BF16),
            vm((2, nz, m // 2 + 16, HD), BF16),
            vm((2, nz, rows // 2, depth), BF16),
            vm((2, nz, rows // 2, wide), BF16),
            vm((2, nz, rows // 2, wide), BF16),
            vm((2, NY, rows // 2, cols), BF16),
            vm((2, NY, rows // 2, cols), BF16),
            dma((10,)),
            dma((2, last)),
            dma((2, last)),
            dma((12,)),
            dma((12,)),
            dma((6,)),
            dma((6,)),
            dma((2, nz)),
            dma((2, nz)),
            dma((2, nz)),
            dma((2, nz)),
            dma((2, nz)),
            dma((2, nz)),
            dma((2, NY)),
            dma((2, NY)),
        ],
        compiler_params=pltpu.CompilerParams(
            collective_id=0, has_side_effects=True, vmem_limit_bytes=60 * 1024 * 1024
        ),
    )(q, pk, pv, nk, nv, ck, cv, rr, cl, w)


def solution(mesh):
    nz = mesh.shape["seq"] // NY
    in_specs = (
        P("seq", "tp"),
        P("seq", "tp"),
        P("seq", "tp"),
        P("seq", "tp"),
        P("seq", "tp"),
        P("seq", None, "tp"),
        P("seq", None, "tp"),
        P("seq"),
        P("seq"),
        P("tp", "seq"),
    )
    return jax.shard_map(
        functools.partial(body, nz),
        mesh=mesh,
        in_specs=in_specs,
        out_specs=P("tp", "seq"),
        check_vma=False,
    )
```

```python
import functools
import math

import jax
import jax.numpy as jnp
from jax import lax
from jax.experimental import pallas as pl
from jax.experimental.pallas import tpu as pltpu
from jax.sharding import PartitionSpec as P

HD = 128
QPG = 8
NY = 4
MESH = pl.DeviceIdType.MESH
SCALE2 = math.log2(math.e) / math.sqrt(HD)
LOG2E = math.log2(math.e)
LOW = -1e30
F32 = jnp.float32
BF16 = jnp.bfloat16


def kernel(
    nz,
    q_ref,
    pk_ref,
    pv_ref,
    nk_ref,
    nv_ref,
    ck_ref,
    cv_ref,
    rr_ref,
    cl_ref,
    w_ref,
    out_ref,
    kbuf,
    vbuf,
    qbuf,
    wbuf,
    ckb,
    cvb,
    nkb,
    nvb,
    rrs,
    cls,
    sca,
    scb,
    acc,
    mst,
    osend,
    orecv,
    lsend,
    lrecv,
    att,
    psend,
    precv,
    fsend,
    frecv,
    loc_sem,
    qs,
    qr,
    ks,
    kr,
    ws,
    wr,
    os_,
    or_,
    ls,
    lr,
    as_,
    ar,
    ps,
    pr,
    fs,
    fr,
):
    nt = nz
    rows = q_ref.shape[0]
    keys = pk_ref.shape[0]
    reqs, slots = ck_ref.shape[0], ck_ref.shape[1]
    depth, cols = w_ref.shape
    last = nz // 2
    s_idx = lax.axis_index("seq")
    t = lax.axis_index("tp")
    z = s_idx // NY
    y = s_idx % NY

    def at_z(v):
        return (lax.rem(v + 2 * nz, nz) * NY + y, t)

    def at_y(v):
        return (z * NY + lax.rem(v + 2 * NY, NY), t)

    def at_t(v):
        return (s_idx, lax.rem(v + 2 * nt, nt))

    def remote(src, dst, ssem, rsem, dev):
        return pltpu.make_async_remote_copy(
            src_ref=src,
            dst_ref=dst,
            send_sem=ssem,
            recv_sem=rsem,
            device_id=dev,
            device_id_type=MESH,
        )

    def greet(dev):
        pl.semaphore_signal(barrier, inc=1, device_id=dev, device_id_type=MESH)

    barrier = pltpu.get_barrier_semaphore()
    greet(at_y(y + 1))
    greet(at_y(y - 1))
    greet(at_z(z + 1))
    greet(at_z(z - 1))
    for i in range(1, nt):
        greet(at_t(t + i))

    local = [
        pltpu.make_async_copy(q_ref, qbuf.at[0], loc_sem.at[0]),
        pltpu.make_async_copy(ck_ref, ckb, loc_sem.at[1]),
        pltpu.make_async_copy(cv_ref, cvb, loc_sem.at[2]),
        pltpu.make_async_copy(nk_ref, nkb.at[pl.ds(0, rows)], loc_sem.at[3]),
        pltpu.make_async_copy(nv_ref, nvb.at[pl.ds(0, rows)], loc_sem.at[4]),
        pltpu.make_async_copy(rr_ref, rrs, loc_sem.at[5]),
        pltpu.make_async_copy(cl_ref, cls, loc_sem.at[6]),
        pltpu.make_async_copy(pk_ref, kbuf.at[0], loc_sem.at[7]),
        pltpu.make_async_copy(pv_ref, vbuf.at[0], loc_sem.at[8]),
        pltpu.make_async_copy(w_ref, wbuf.at[y], loc_sem.at[9]),
    ]
    pl.semaphore_wait(barrier, nt + 3)

    lo, hi = pl.ds(0, keys // 2), pl.ds(keys // 2, keys // 2)
    ways = (at_y(y + 1), at_y(y - 1))
    place = (lo, hi)

    def kv_copy(stage, way, which):
        buf = (kbuf, vbuf)[which]
        whole = (pk_ref, pv_ref)[which]
        sem = (stage - 1) * 4 + way * 2 + which
        if stage == 1:
            src = whole.at[place[way]]
        elif stage == 2:
            src = whole.at[place[1 - way]]
        else:
            src = buf.at[1, place[way]]
        return remote(src, buf.at[stage, place[way]], ks.at[sem], kr.at[sem], ways[way])

    def kv_stage(stage, act):
        for which in range(2):
            for way in range(2):
                act(kv_copy(stage, way, which))

    kv_stage(1, lambda c: c.start())

    half = rows // 2
    halves = (pl.ds(0, half), pl.ds(half, half))
    zways = (at_z(z + 1), at_z(z - 1))

    def q_slot(way, k):
        return 2 * k - 1 if (way == 0 or k == last) else 2 * k

    def q_copy(way, k):
        dst = qbuf.at[q_slot(way, k)]
        src = q_ref if k == 1 else qbuf.at[q_slot(way, k - 1)]
        if k == last:
            src, dst = src.at[halves[way]], dst.at[halves[way]]
        return remote(src, dst, qs.at[way, k - 1], qr.at[way, k - 1], zways[way])

    for way in range(2):
        q_copy(way, 1).start()
    for c in (local[0], local[7], local[8]):
        c.start()

    def queries_of(i, first=0, parts=2):
        return jnp.concatenate(
            [
                qbuf[i, c * half : (c + 1) * half, h * HD : (h + 1) * HD]
                for c in range(first, first + parts)
                for h in range(QPG)
            ],
            axis=0,
        )

    def per_head(bias):
        return jnp.concatenate([bias[:half]] * QPG + [bias[half:]] * QPG, axis=0)

    def scores(q, k):
        return lax.dot_general(q, k, (((1,), (1,)), ((), ())), preferred_element_type=F32)

    def with_ones(v):
        return jnp.concatenate([v, jnp.ones_like(v)], axis=1)

    for i in range(nz):
        acc[i] = jnp.zeros((rows * QPG, 2 * HD), F32)
        mst[i] = jnp.full((rows * QPG, HD), LOW, F32)

    mh = half * QPG

    def fill(buf, blk, picks):
        q = jnp.concatenate([queries_of(i, f, n) for i, f, n in picks], axis=0)
        buf[...] = scores(q, kbuf[blk])

    def absorb(buf, blk, picks):
        ws_, alphas = [], []
        at = 0
        for i, f, n in picks:
            m = n * mh
            own = pl.ds(f * mh, m)
            chunks = [buf[at : at + m, c * HD : (c + 1) * HD] for c in range(keys // HD)]
            at += m
            m_old = mst[i, own]
            m_new = jnp.maximum(
                m_old, functools.reduce(jnp.maximum, chunks).max(axis=1, keepdims=True)
            )
            m2 = m_new * SCALE2
            ws_.append(
                jnp.concatenate([jnp.exp2(c * SCALE2 - m2).astype(BF16) for c in chunks], axis=1)
            )
            alphas.append(jnp.exp2(m_old * SCALE2 - m2))
            mst[i, own] = m_new
        o = jnp.dot(
            jnp.concatenate(ws_, axis=0), with_ones(vbuf[blk]), preferred_element_type=F32
        )
        at = 0
        for (i, f, n), alpha in zip(picks, alphas):
            m = n * mh
            own = pl.ds(f * mh, m)
            acc[i, own] = acc[i, own] * jnp.concatenate([alpha, alpha], axis=1) + o[at : at + m]
            at += m

    late = max(last - 2, 0)
    early = list(range(late))
    order = [(0, p) for p in early[:2]] + [(1, p) for p in early[:2]]
    for p in early[2:]:
        order += [(0, p), (1, p)]
    tail = list(range(late, last))
    if tail:
        order += [(0, tail[0]), (1, tail[0])]
    order += [(2, p) for p in early + tail[:1]]
    for p in tail[1:]:
        order += [(0, p), (1, p), (2, p)]
    need_q = {}
    for n, (b, p) in enumerate(order):
        need_q.setdefault(p, n)
    need_b = {b: min(n for n, o in enumerate(order) if o[0] == b) for b in (0, 1, 2)}

    def waits(n):
        def when(cond, act):
            if isinstance(n, int):
                if n == cond:
                    act()
            else:
                pl.when(n == cond)(act)

        def q_step(k):
            for way in range(2):
                q_copy(way, k).wait_recv()
                if k < last:
                    q_copy(way, k + 1).start()

        def own():
            for c in (local[0], local[7], local[8]):
                c.wait()

        def blk1():
            for which in range(2):
                for way in range(2):
                    kv_copy(1, way, which).wait_recv()
                    kv_copy(3, way, which).start()

        when(need_b[0], own)
        for p in range(last):
            when(need_q[p], lambda p=p: q_step(p + 1))
        when(need_b[1], blk1)
        when(need_b[2], lambda: kv_stage(2, lambda c: c.wait_recv()))

    def tile(n):
        if isinstance(n, int):
            b, p = order[n]
        else:
            b = p = 0
            for m, (bb, pp) in enumerate(order):
                b = jnp.where(n == m, bb, b)
                p = jnp.where(n == m, pp, p)
        return b, [(2 * p, 0, 2), (2 * p + 1, 0, 2)]

    count = len(order)
    waits(0)
    fill(sca, *tile(0))
    kv_stage(2, lambda c: c.start())
    for c in local[1:7] + local[9:]:
        c.start()

    def step(m, carry):
        for buf, other, n in ((sca, scb, 2 * m), (scb, sca, 2 * m + 1)):
            waits(n + 1)
            fill(other, *tile(n + 1))
            absorb(buf, *tile(n))
        return carry

    pairs = (count - 1) // 2
    lax.fori_loop(0, pairs, step, 0)
    rest = list(range(2 * pairs, count))
    bufs = (sca, scb)
    for n in rest:
        if n + 1 < count:
            waits(n + 1)
            fill(bufs[(n + 1) % 2], *tile(n + 1))
        absorb(bufs[n % 2], *tile(n))

    wlo, whi = pl.ds(0, depth // 2), pl.ds(depth // 2, depth // 2)
    wplace = (wlo, whi)
    origin = (lax.rem(y + NY - 1, NY), lax.rem(y + 1, NY))

    def w_copy(stage, way):
        sem = (stage - 1) * 2 + way
        if stage == 3:
            src = dst = wbuf.at[origin[way], wplace[way]]
        else:
            part = wplace[way] if stage == 1 else wplace[1 - way]
            src, dst = w_ref.at[part], wbuf.at[y, part]
        return remote(src, dst, ws.at[sem], wr.at[sem], ways[way])

    def w_stage(stage, act):
        for way in range(2):
            act(w_copy(stage, way))

    lane8 = lax.broadcasted_iota(jnp.int32, (8, HD), 1)
    groups = half // 8

    staged = nz == 8

    def o_dest(c, i):
        if staged and i == 7:
            return at_z(z - 2) if c == 0 else at_z(z + 2)
        if staged and i > 4:
            return at_z(z - 1) if i == 5 else at_z(z + 1)
        return at_z(z - (i + 1) // 2) if i % 2 else at_z(z + i // 2)

    def o_copy(c, i):
        return remote(osend.at[c, i], orecv.at[c, i], os_.at[c, i], or_.at[c, i], o_dest(c, i))

    def l_copy(c, i):
        return remote(lsend.at[c, i], lrecv.at[c, i], ls.at[c, i], lr.at[c, i], o_dest(c, i))

    def o_start(c, i):
        o_copy(c, i).start()
        l_copy(c, i).start()

    def o_wait(c, i):
        o_copy(c, i).wait_recv()
        l_copy(c, i).wait_recv()

    def finish(c, i):
        own = pl.ds(c * mh, mh)
        a = acc[i, own]
        l = a[:, HD:]
        osend[c, i] = (a[:, :HD] / l).astype(BF16)
        m = mst[i, own]
        top_of = jnp.zeros((8, HD), F32)
        sum_of = jnp.ones((8, HD), F32)
        for h in range(QPG):
            for g in range(groups):
                r0 = h * half + g * 8
                pick = lane8 == g * 8 + h
                top_of = jnp.where(pick, m[r0 : r0 + 8, :], top_of)
                sum_of = jnp.where(pick, l[r0 : r0 + 8, :], sum_of)
        packed = top_of * SCALE2 + jnp.log(sum_of) * LOG2E
        rolled = pltpu.roll(packed, 0, 1, stride=16, stride_axis=0)
        lsend[c, i] = jnp.sum(rolled, axis=0, keepdims=True)

    finals = []
    for top_slot, low_slot in ((nz, nz // 2), (nz // 2, 0)):
        for c in range(2):
            finals.append((c, [(i, c, 1) for i in range(top_slot - 1, low_slot - 1, -1)]))

    def part(n):
        return (sca, scb)[n % 2].at[pl.ds(0, len(finals[n][1]) * mh)]

    for way in range(2):
        kv_copy(3, way, 0).wait_recv()
    fill(part(0), 3, finals[0][1])
    for way in range(2):
        kv_copy(3, way, 1).wait_recv()
    for n, (c, picks) in enumerate(finals):
        if n + 1 < len(finals):
            fill(part(n + 1), 3, finals[n + 1][1])
        absorb(part(n), 3, picks)
        for i, _, _ in picks:
            if i > 0:
                finish(c, i)
                if not (staged and i in (3, 4)):
                    o_start(c, i)
        if n == 0:
            w_stage(1, lambda c: c.start())
        if n == 2:
            w_stage(2, lambda c: c.start())

    pad = nkb.shape[0]
    nkb[pl.ds(rows, pad - rows), :] = jnp.zeros((pad - rows, HD), BF16)
    nvb[pl.ds(rows, pad - rows), :] = jnp.zeros((pad - rows, HD), BF16)
    for c in local[1:7]:
        c.wait()
    sub = lax.broadcasted_iota(jnp.int32, (rows, pad), 0)
    lane = lax.broadcasted_iota(jnp.int32, (rows, pad), 1)
    rr_col = jnp.zeros((rows, pad), jnp.int32)
    rr_row = jnp.zeros((rows, pad), jnp.int32)
    for r in range(rows):
        req = rrs[r] - s_idx * reqs
        rr_col = jnp.where(sub == r, req, rr_col)
        rr_row = jnp.where(lane == r, req, rr_row)

    q_own = queries_of(0)
    parts = []
    for j in range(reqs):
        biases = [
            jnp.where((rr_col == j) & (lane + c * pad < cls[j]), 0.0, LOW).astype(F32)
            for c in range(slots // pad)
        ]
        bias = jnp.concatenate(biases, axis=1)
        parts.append(scores(q_own, ckb[j]) + per_head(bias))
    bias = jnp.where((rr_row == rr_col) & (lane <= sub), 0.0, LOW).astype(F32)
    parts.append(scores(q_own, nkb[...]) + per_head(bias))
    top = functools.reduce(jnp.maximum, [p.max(axis=1, keepdims=True) for p in parts])
    total = jnp.zeros((rows * QPG, 2 * HD), F32)
    for j, p in enumerate(parts):
        w = jnp.exp2((p - top) * SCALE2).astype(BF16)
        v = cvb[j] if j < reqs else nvb[...]
        total = total + jnp.dot(w, with_ones(v), preferred_element_type=F32)
    top = jnp.broadcast_to(top, (rows * QPG, HD))
    m_old = mst[0]
    m_new = jnp.maximum(m_old, top)
    keep = jnp.exp2((m_old - m_new) * SCALE2)
    add = jnp.exp2((top - m_new) * SCALE2)
    acc[0] = acc[0] * jnp.concatenate([keep, keep], axis=1) + total * jnp.concatenate(
        [add, add], axis=1
    )
    mst[0] = m_new
    for c in range(2):
        finish(c, 0)

    far_first = sorted(range(1, nz), key=lambda d: -min(d, nz - d))

    def a_copy(c, d):
        ref = att.at[c, z]
        return remote(ref, ref, as_.at[c, d], ar.at[c, d], at_z(z + d))

    sub8 = lax.broadcasted_iota(jnp.int32, (8, HD), 0)

    def spread(row):
        row = jnp.broadcast_to(row, (8, HD))
        out = row
        for k in range(1, 8):
            out = jnp.where(sub8 == k, pltpu.roll(row, HD - 16 * k, 1), out)
        return out

    def weights(c, sources):
        lses = [lsend[c, i] if own else lrecv[c, i] for own, i in sources]
        best = functools.reduce(jnp.maximum, lses)
        wts = [jnp.exp2(v - best) for v in lses]
        norm = functools.reduce(jnp.add, wts)
        return [spread(v / norm) for v in wts], best + jnp.log(norm) * LOG2E

    def blend(c, sources, wts, h):
        tot = jnp.zeros((half, HD), F32)
        for (own, i), w in zip(sources, wts):
            o = (osend if own else orecv)[c, i, h * half : (h + 1) * half, :].astype(F32)
            col = jnp.concatenate(
                [w[:, g * 8 + h : g * 8 + h + 1] for g in range(groups)], axis=0
            )
            tot = tot + o * col
        return tot.astype(BF16)

    def join(c):
        o_wait(c, 5)
        o_wait(c, 6)
        o_wait(c, 7)
        for i, extra in ((3, 5), (4, 6)):
            sources = [(True, i), (False, extra)]
            if i == 3 + c:
                sources.append((False, 7))
            wts, lse = weights(c, sources)
            for h in range(QPG):
                osend[c, i, h * half : (h + 1) * half, :] = blend(c, sources, wts, h)
            lsend[c, i] = lse
            o_start(c, i)

    def merge(c):
        arriving = range(1, 5) if staged else range(1, nz)
        for i in arriving:
            o_wait(c, i)
        sources = [(True, 0)] + [(False, i) for i in arriving]
        wts, _ = weights(c, sources)
        for h in range(QPG):
            att[c, z, :, h * HD : (h + 1) * HD] = blend(c, sources, wts, h)
        for d in far_first:
            a_copy(c, d).start()

    if staged:
        join(0)
        join(1)
    merge(0)
    merge(1)
    w_stage(1, lambda c: c.wait_recv())
    w_stage(3, lambda c: c.start())

    local[9].wait()
    w_stage(2, lambda c: c.wait_recv())
    w_stage(3, lambda c: c.wait_recv())

    def p_copy(c, e):
        dst_t = lax.rem(t + e, nt)
        return remote(psend.at[c, dst_t], precv.at[c, e], ps.at[c, e], pr.at[c, e], at_t(t + e))

    for c in range(2):
        for d in far_first:
            a_copy(c, d).wait_recv()
        a_all = att[c].reshape(nz * half, depth)
        for j in range(NY):
            out = jnp.dot(a_all, wbuf[j], preferred_element_type=F32).astype(BF16)
            psend[c, :, :, j * cols : (j + 1) * cols] = out.reshape(nz, half, cols)
        for e in range(1, nt):
            p_copy(c, e).start()

    def f_copy(c, e):
        dst_y = lax.rem(y + e, NY)
        return remote(fsend.at[c, dst_y], frecv.at[c, y], fs.at[c, e], fr.at[c, e], at_y(y + e))

    for way in range(2):
        for k in range(1, last + 1):
            q_copy(way, k).wait_send()
    for stage in (1, 2, 3):
        kv_stage(stage, lambda c: c.wait_send())
        w_stage(stage, lambda c: c.wait_send())
    for c in range(2):
        for i in range(1, nz):
            o_copy(c, i).wait_send()
            l_copy(c, i).wait_send()
            a_copy(c, i).wait_send()

    for c in range(2):
        tot = psend[c, t].astype(F32)
        for e in range(1, nt):
            p_copy(c, e).wait_recv()
            tot = tot + precv[c, e].astype(F32)
        tot = tot.astype(BF16)
        for j in range(NY):
            fsend[c, j] = tot[:, j * cols : (j + 1) * cols]
        for e in range(1, NY):
            f_copy(c, e).start()
        frecv[c, y] = fsend[c, y]
    for c in range(2):
        for e in range(1, NY):
            f_copy(c, e).wait_recv()
        for j in range(NY):
            out_ref[j * rows + c * half : j * rows + (c + 1) * half, :] = frecv[c, j]

    for c in range(2):
        for e in range(1, nt):
            p_copy(c, e).wait_send()
        for e in range(1, NY):
            f_copy(c, e).wait_send()


def body(nz, q, pk, pv, nk, nv, ck, cv, rr, cl, w):
    rows = q.shape[0]
    feat = q.shape[1]
    keys = pk.shape[0]
    reqs, slots = ck.shape[0], ck.shape[1]
    depth, cols = w.shape
    m = rows * QPG
    wide = NY * cols
    last = nz // 2
    vm = pltpu.VMEM
    dma = pltpu.SemaphoreType.DMA
    any_spec = pl.BlockSpec(memory_space=pl.ANY)
    vmem_spec = pl.BlockSpec(memory_space=pltpu.VMEM)
    return pl.pallas_call(
        functools.partial(kernel, nz),
        out_shape=jax.ShapeDtypeStruct((NY * rows, cols), BF16),
        in_specs=[any_spec] * 10,
        out_specs=vmem_spec,
        scratch_shapes=[
            vm((NY, keys, HD), BF16),
            vm((NY, keys, HD), BF16),
            vm((nz, rows, feat), BF16),
            vm((NY, depth, cols), BF16),
            vm((reqs, slots, HD), BF16),
            vm((reqs, slots, HD), BF16),
            vm((HD, HD), BF16),
            vm((HD, HD), BF16),
            pltpu.SMEM((rows,), jnp.int32),
            pltpu.SMEM((reqs,), jnp.int32),
            vm((2 * m, keys), F32),
            vm((2 * m, keys), F32),
            vm((nz, m, 2 * HD), F32),
            vm((nz, m, HD), F32),
            vm((2, nz, m // 2, HD), BF16),
            vm((2, nz, m // 2, HD), BF16),
            vm((2, nz, 1, HD), F32),
            vm((2, nz, 1, HD), F32),
            vm((2, nz, rows // 2, depth), BF16),
            vm((2, nz, rows // 2, wide), BF16),
            vm((2, nz, rows // 2, wide), BF16),
            vm((2, NY, rows // 2, cols), BF16),
            vm((2, NY, rows // 2, cols), BF16),
            dma((10,)),
            dma((2, last)),
            dma((2, last)),
            dma((12,)),
            dma((12,)),
            dma((6,)),
            dma((6,)),
            dma((2, nz)),
            dma((2, nz)),
            dma((2, nz)),
            dma((2, nz)),
            dma((2, nz)),
            dma((2, nz)),
            dma((2, nz)),
            dma((2, nz)),
            dma((2, NY)),
            dma((2, NY)),
        ],
        compiler_params=pltpu.CompilerParams(
            collective_id=0, has_side_effects=True, vmem_limit_bytes=60 * 1024 * 1024
        ),
    )(q, pk, pv, nk, nv, ck, cv, rr, cl, w)


def solution(mesh):
    nz = mesh.shape["seq"] // NY
    in_specs = (
        P("seq", "tp"),
        P("seq", "tp"),
        P("seq", "tp"),
        P("seq", "tp"),
        P("seq", "tp"),
        P("seq", None, "tp"),
        P("seq", None, "tp"),
        P("seq"),
        P("seq"),
        P("tp", "seq"),
    )
    return jax.shard_map(
        functools.partial(body, nz),
        mesh=mesh,
        in_specs=in_specs,
        out_specs=P("tp", "seq"),
        check_vma=False,
    )
```

```python
import functools
import math

import jax
import jax.numpy as jnp
from jax import lax
from jax.experimental import pallas as pl
from jax.experimental.pallas import tpu as pltpu
from jax.sharding import PartitionSpec as P

HD = 128
QPG = 8
NY = 4
MESH = pl.DeviceIdType.MESH
SCALE2 = math.log2(math.e) / math.sqrt(HD)
LOG2E = math.log2(math.e)
LOW = -1e30
F32 = jnp.float32
BF16 = jnp.bfloat16


def kernel(
    nz,
    q_ref,
    pk_ref,
    pv_ref,
    nk_ref,
    nv_ref,
    ck_ref,
    cv_ref,
    rr_ref,
    cl_ref,
    w_ref,
    out_ref,
    kbuf,
    vbuf,
    qbuf,
    wbuf,
    ckb,
    cvb,
    nkb,
    nvb,
    rrs,
    cls,
    sca,
    scb,
    acc,
    mst,
    osend,
    orecv,
    lsend,
    lrecv,
    att,
    psend,
    precv,
    fsend,
    frecv,
    loc_sem,
    qs,
    qr,
    ks,
    kr,
    ws,
    wr,
    os_,
    or_,
    ls,
    lr,
    as_,
    ar,
    ps,
    pr,
    fs,
    fr,
):
    nt = nz
    rows = q_ref.shape[0]
    keys = pk_ref.shape[0]
    reqs, slots = ck_ref.shape[0], ck_ref.shape[1]
    depth, cols = w_ref.shape
    last = nz // 2
    s_idx = lax.axis_index("seq")
    t = lax.axis_index("tp")
    z = s_idx // NY
    y = s_idx % NY

    def at_z(v):
        return (lax.rem(v + 2 * nz, nz) * NY + y, t)

    def at_y(v):
        return (z * NY + lax.rem(v + 2 * NY, NY), t)

    def at_t(v):
        return (s_idx, lax.rem(v + 2 * nt, nt))

    def remote(src, dst, ssem, rsem, dev):
        return pltpu.make_async_remote_copy(
            src_ref=src,
            dst_ref=dst,
            send_sem=ssem,
            recv_sem=rsem,
            device_id=dev,
            device_id_type=MESH,
        )

    def greet(dev):
        pl.semaphore_signal(barrier, inc=1, device_id=dev, device_id_type=MESH)

    barrier = pltpu.get_barrier_semaphore()
    greet(at_y(y + 1))
    greet(at_y(y - 1))
    greet(at_z(z + 1))
    greet(at_z(z - 1))
    if nz == 8:
        greet(at_z(z + 2))
        greet(at_z(z - 2))
    for i in range(1, nt):
        greet(at_t(t + i))

    local = [
        pltpu.make_async_copy(q_ref, qbuf.at[0], loc_sem.at[0]),
        pltpu.make_async_copy(ck_ref, ckb, loc_sem.at[1]),
        pltpu.make_async_copy(cv_ref, cvb, loc_sem.at[2]),
        pltpu.make_async_copy(nk_ref, nkb.at[pl.ds(0, rows)], loc_sem.at[3]),
        pltpu.make_async_copy(nv_ref, nvb.at[pl.ds(0, rows)], loc_sem.at[4]),
        pltpu.make_async_copy(rr_ref, rrs, loc_sem.at[5]),
        pltpu.make_async_copy(cl_ref, cls, loc_sem.at[6]),
        pltpu.make_async_copy(pk_ref, kbuf.at[0], loc_sem.at[7]),
        pltpu.make_async_copy(pv_ref, vbuf.at[0], loc_sem.at[8]),
        pltpu.make_async_copy(w_ref, wbuf.at[y], loc_sem.at[9]),
    ]
    pl.semaphore_wait(barrier, nt + (5 if nz == 8 else 3))

    lo, hi = pl.ds(0, keys // 2), pl.ds(keys // 2, keys // 2)
    ways = (at_y(y + 1), at_y(y - 1))
    place = (lo, hi)

    def kv_copy(stage, way, which):
        buf = (kbuf, vbuf)[which]
        whole = (pk_ref, pv_ref)[which]
        sem = (stage - 1) * 4 + way * 2 + which
        if stage == 1:
            src = whole.at[place[way]]
        elif stage == 2:
            src = whole.at[place[1 - way]]
        else:
            src = buf.at[1, place[way]]
        return remote(src, buf.at[stage, place[way]], ks.at[sem], kr.at[sem], ways[way])

    def kv_stage(stage, act):
        for which in range(2):
            for way in range(2):
                act(kv_copy(stage, way, which))

    kv_stage(1, lambda c: c.start())

    half = rows // 2
    halves = (pl.ds(0, half), pl.ds(half, half))
    reach = 2 if nz == 8 else 1

    def q_slot(way, k):
        return 2 * k - 1 if (way == 0 or k == last) else 2 * k

    def q_copy(way, k):
        dst = qbuf.at[q_slot(way, k)]
        src = q_ref if k <= reach else qbuf.at[q_slot(way, reach)]
        step = k if k <= reach else k - reach
        if k == last:
            src, dst = src.at[halves[way]], dst.at[halves[way]]
        return remote(src, dst, qs.at[way, k - 1], qr.at[way, k - 1], at_z(z + step if way == 0 else z - step))

    for k in range(1, min(reach, last) + 1):
        for way in range(2):
            q_copy(way, k).start()
    for c in (local[0], local[7], local[8]):
        c.start()

    def queries_of(i, first=0, parts=2):
        return jnp.concatenate(
            [
                qbuf[i, c * half : (c + 1) * half, h * HD : (h + 1) * HD]
                for c in range(first, first + parts)
                for h in range(QPG)
            ],
            axis=0,
        )

    def per_head(bias):
        return jnp.concatenate([bias[:half]] * QPG + [bias[half:]] * QPG, axis=0)

    def scores(q, k):
        return lax.dot_general(q, k, (((1,), (1,)), ((), ())), preferred_element_type=F32)

    def with_ones(v):
        return jnp.concatenate([v, jnp.ones_like(v)], axis=1)

    for i in range(nz):
        acc[i] = jnp.zeros((rows * QPG, 2 * HD), F32)
        mst[i] = jnp.full((rows * QPG, HD), LOW, F32)

    mh = half * QPG

    def fill(buf, blk, picks):
        q = jnp.concatenate([queries_of(i, f, n) for i, f, n in picks], axis=0)
        buf[...] = scores(q, kbuf[blk])

    def absorb(buf, blk, picks):
        ws_, alphas = [], []
        at = 0
        for i, f, n in picks:
            m = n * mh
            own = pl.ds(f * mh, m)
            chunks = [buf[at : at + m, c * HD : (c + 1) * HD] for c in range(keys // HD)]
            at += m
            m_old = mst[i, own]
            m_new = jnp.maximum(
                m_old, functools.reduce(jnp.maximum, chunks).max(axis=1, keepdims=True)
            )
            m2 = m_new * SCALE2
            ws_.append(
                jnp.concatenate([jnp.exp2(c * SCALE2 - m2).astype(BF16) for c in chunks], axis=1)
            )
            alphas.append(jnp.exp2(m_old * SCALE2 - m2))
            mst[i, own] = m_new
        o = jnp.dot(
            jnp.concatenate(ws_, axis=0), with_ones(vbuf[blk]), preferred_element_type=F32
        )
        at = 0
        for (i, f, n), alpha in zip(picks, alphas):
            m = n * mh
            own = pl.ds(f * mh, m)
            acc[i, own] = acc[i, own] * jnp.concatenate([alpha, alpha], axis=1) + o[at : at + m]
            at += m

    late = max(last - 2, 0)
    early = list(range(late))
    order = [(0, p) for p in early[:2]] + [(1, p) for p in early[:2]]
    for p in early[2:]:
        order += [(0, p), (1, p)]
    tail = list(range(late, last))
    if tail:
        order += [(0, tail[0]), (1, tail[0])]
    order += [(2, p) for p in early + tail[:1]]
    for p in tail[1:]:
        order += [(0, p), (1, p), (2, p)]
    need_q = {}
    for n, (b, p) in enumerate(order):
        need_q.setdefault(p, n)
    need_b = {b: min(n for n, o in enumerate(order) if o[0] == b) for b in (0, 1, 2)}

    def waits(n):
        def when(cond, act):
            if isinstance(n, int):
                if n == cond:
                    act()
            else:
                pl.when(n == cond)(act)

        def q_step(k):
            for way in range(2):
                q_copy(way, k).wait_recv()
            if k == reach:
                for far in range(last, reach, -1):
                    for way in range(2):
                        q_copy(way, far).start()

        def own():
            for c in (local[0], local[7], local[8]):
                c.wait()

        def blk1():
            for which in range(2):
                for way in range(2):
                    kv_copy(1, way, which).wait_recv()
                    kv_copy(3, way, which).start()

        when(need_b[0], own)
        for p in range(last):
            when(need_q[p], lambda p=p: q_step(p + 1))
        when(need_b[1], blk1)
        when(need_b[2], lambda: kv_stage(2, lambda c: c.wait_recv()))

    def tile(n):
        if isinstance(n, int):
            b, p = order[n]
        else:
            b = p = 0
            for m, (bb, pp) in enumerate(order):
                b = jnp.where(n == m, bb, b)
                p = jnp.where(n == m, pp, p)
        return b, [(2 * p, 0, 2), (2 * p + 1, 0, 2)]

    count = len(order)
    waits(0)
    fill(sca, *tile(0))
    kv_stage(2, lambda c: c.start())
    for c in local[1:7] + local[9:]:
        c.start()

    def step(m, carry):
        for buf, other, n in ((sca, scb, 2 * m), (scb, sca, 2 * m + 1)):
            waits(n + 1)
            fill(other, *tile(n + 1))
            absorb(buf, *tile(n))
        return carry

    pairs = (count - 1) // 2
    lax.fori_loop(0, pairs, step, 0)
    rest = list(range(2 * pairs, count))
    bufs = (sca, scb)
    for n in rest:
        if n + 1 < count:
            waits(n + 1)
            fill(bufs[(n + 1) % 2], *tile(n + 1))
        absorb(bufs[n % 2], *tile(n))

    wlo, whi = pl.ds(0, depth // 2), pl.ds(depth // 2, depth // 2)
    wplace = (wlo, whi)
    origin = (lax.rem(y + NY - 1, NY), lax.rem(y + 1, NY))

    def w_copy(stage, way):
        sem = (stage - 1) * 2 + way
        if stage == 3:
            src = dst = wbuf.at[origin[way], wplace[way]]
        else:
            part = wplace[way] if stage == 1 else wplace[1 - way]
            src, dst = w_ref.at[part], wbuf.at[y, part]
        return remote(src, dst, ws.at[sem], wr.at[sem], ways[way])

    def w_stage(stage, act):
        for way in range(2):
            act(w_copy(stage, way))

    lane8 = lax.broadcasted_iota(jnp.int32, (8, HD), 1)
    groups = half // 8

    staged = nz == 8

    def o_dest(c, i):
        if staged and i == 7:
            return at_z(z - 2) if c == 0 else at_z(z + 2)
        if staged and i > 4:
            return at_z(z - 1) if i == 5 else at_z(z + 1)
        return at_z(z - (i + 1) // 2) if i % 2 else at_z(z + i // 2)

    def o_copy(c, i):
        return remote(osend.at[c, i], orecv.at[c, i], os_.at[c, i], or_.at[c, i], o_dest(c, i))

    def l_copy(c, i):
        return remote(lsend.at[c, i], lrecv.at[c, i], ls.at[c, i], lr.at[c, i], o_dest(c, i))

    def o_start(c, i):
        o_copy(c, i).start()
        l_copy(c, i).start()

    def o_wait(c, i):
        o_copy(c, i).wait_recv()
        l_copy(c, i).wait_recv()

    def finish(c, i):
        own = pl.ds(c * mh, mh)
        a = acc[i, own]
        l = a[:, HD:]
        osend[c, i] = (a[:, :HD] / l).astype(BF16)
        m = mst[i, own]
        top_of = jnp.zeros((8, HD), F32)
        sum_of = jnp.ones((8, HD), F32)
        for h in range(QPG):
            for g in range(groups):
                r0 = h * half + g * 8
                pick = lane8 == g * 8 + h
                top_of = jnp.where(pick, m[r0 : r0 + 8, :], top_of)
                sum_of = jnp.where(pick, l[r0 : r0 + 8, :], sum_of)
        packed = top_of * SCALE2 + jnp.log(sum_of) * LOG2E
        rolled = pltpu.roll(packed, 0, 1, stride=16, stride_axis=0)
        lsend[c, i] = jnp.sum(rolled, axis=0, keepdims=True)

    finals = []
    for top_slot, low_slot in ((nz, nz // 2), (nz // 2, 0)):
        for c in range(2):
            finals.append((c, [(i, c, 1) for i in range(top_slot - 1, low_slot - 1, -1)]))

    def part(n):
        return (sca, scb)[n % 2].at[pl.ds(0, len(finals[n][1]) * mh)]

    for way in range(2):
        kv_copy(3, way, 0).wait_recv()
    fill(part(0), 3, finals[0][1])
    for way in range(2):
        kv_copy(3, way, 1).wait_recv()
    for n, (c, picks) in enumerate(finals):
        if n + 1 < len(finals):
            fill(part(n + 1), 3, finals[n + 1][1])
        absorb(part(n), 3, picks)
        for i, _, _ in picks:
            if i > 0:
                finish(c, i)
                if not (staged and i in (3, 4)):
                    o_start(c, i)
        if n == 0:
            w_stage(1, lambda c: c.start())
        if n == 2:
            w_stage(2, lambda c: c.start())

    pad = nkb.shape[0]
    nkb[pl.ds(rows, pad - rows), :] = jnp.zeros((pad - rows, HD), BF16)
    nvb[pl.ds(rows, pad - rows), :] = jnp.zeros((pad - rows, HD), BF16)
    for c in local[1:7]:
        c.wait()
    sub = lax.broadcasted_iota(jnp.int32, (rows, pad), 0)
    lane = lax.broadcasted_iota(jnp.int32, (rows, pad), 1)
    rr_col = jnp.zeros((rows, pad), jnp.int32)
    rr_row = jnp.zeros((rows, pad), jnp.int32)
    for r in range(rows):
        req = rrs[r] - s_idx * reqs
        rr_col = jnp.where(sub == r, req, rr_col)
        rr_row = jnp.where(lane == r, req, rr_row)

    q_own = queries_of(0)
    parts = []
    for j in range(reqs):
        biases = [
            jnp.where((rr_col == j) & (lane + c * pad < cls[j]), 0.0, LOW).astype(F32)
            for c in range(slots // pad)
        ]
        bias = jnp.concatenate(biases, axis=1)
        parts.append(scores(q_own, ckb[j]) + per_head(bias))
    bias = jnp.where((rr_row == rr_col) & (lane <= sub), 0.0, LOW).astype(F32)
    parts.append(scores(q_own, nkb[...]) + per_head(bias))
    top = functools.reduce(jnp.maximum, [p.max(axis=1, keepdims=True) for p in parts])
    total = jnp.zeros((rows * QPG, 2 * HD), F32)
    for j, p in enumerate(parts):
        w = jnp.exp2((p - top) * SCALE2).astype(BF16)
        v = cvb[j] if j < reqs else nvb[...]
        total = total + jnp.dot(w, with_ones(v), preferred_element_type=F32)
    top = jnp.broadcast_to(top, (rows * QPG, HD))
    m_old = mst[0]
    m_new = jnp.maximum(m_old, top)
    keep = jnp.exp2((m_old - m_new) * SCALE2)
    add = jnp.exp2((top - m_new) * SCALE2)
    acc[0] = acc[0] * jnp.concatenate([keep, keep], axis=1) + total * jnp.concatenate(
        [add, add], axis=1
    )
    mst[0] = m_new
    for c in range(2):
        finish(c, 0)

    far_first = sorted(range(1, nz), key=lambda d: -min(d, nz - d))

    def a_copy(c, d):
        ref = att.at[c, z]
        return remote(ref, ref, as_.at[c, d], ar.at[c, d], at_z(z + d))

    sub8 = lax.broadcasted_iota(jnp.int32, (8, HD), 0)

    def spread(row):
        row = jnp.broadcast_to(row, (8, HD))
        out = row
        for k in range(1, 8):
            out = jnp.where(sub8 == k, pltpu.roll(row, HD - 16 * k, 1), out)
        return out

    def weights(c, sources):
        lses = [lsend[c, i] if own else lrecv[c, i] for own, i in sources]
        best = functools.reduce(jnp.maximum, lses)
        wts = [jnp.exp2(v - best) for v in lses]
        norm = functools.reduce(jnp.add, wts)
        return [spread(v / norm) for v in wts], best + jnp.log(norm) * LOG2E

    def blend(c, sources, wts, h):
        tot = jnp.zeros((half, HD), F32)
        for (own, i), w in zip(sources, wts):
            o = (osend if own else orecv)[c, i, h * half : (h + 1) * half, :].astype(F32)
            col = jnp.concatenate(
                [w[:, g * 8 + h : g * 8 + h + 1] for g in range(groups)], axis=0
            )
            tot = tot + o * col
        return tot.astype(BF16)

    def join(c):
        for i in (4 - c, 3 + c):
            sources = [(True, i), (False, i + 2)]
            if i == 3 + c:
                sources.append((False, 7))
            for _, extra in sources[1:]:
                o_wait(c, extra)
            wts, lse = weights(c, sources)
            for h in range(QPG):
                osend[c, i, h * half : (h + 1) * half, :] = blend(c, sources, wts, h)
            lsend[c, i] = lse
            o_start(c, i)

    def merge(c):
        arriving = range(1, 5) if staged else range(1, nz)
        for i in arriving:
            o_wait(c, i)
        sources = [(True, 0)] + [(False, i) for i in arriving]
        wts, _ = weights(c, sources)
        for h in range(QPG):
            att[c, z, :, h * HD : (h + 1) * HD] = blend(c, sources, wts, h)
        for d in far_first:
            a_copy(c, d).start()

    if staged:
        join(0)
        join(1)
    merge(0)
    merge(1)
    w_stage(1, lambda c: c.wait_recv())
    w_stage(3, lambda c: c.start())

    local[9].wait()
    w_stage(2, lambda c: c.wait_recv())
    w_stage(3, lambda c: c.wait_recv())

    def p_copy(c, e):
        dst_t = lax.rem(t + e, nt)
        return remote(psend.at[c, dst_t], precv.at[c, e], ps.at[c, e], pr.at[c, e], at_t(t + e))

    for c in range(2):
        for d in far_first:
            a_copy(c, d).wait_recv()
        a_all = att[c].reshape(nz * half, depth)
        for j in range(NY):
            out = jnp.dot(a_all, wbuf[j], preferred_element_type=F32).astype(BF16)
            psend[c, :, :, j * cols : (j + 1) * cols] = out.reshape(nz, half, cols)
        for e in sorted(range(1, nt), key=lambda e: -min(e, nt - e)):
            p_copy(c, e).start()

    def f_copy(c, e):
        dst_y = lax.rem(y + e, NY)
        return remote(fsend.at[c, dst_y], frecv.at[c, y], fs.at[c, e], fr.at[c, e], at_y(y + e))

    for way in range(2):
        for k in range(1, last + 1):
            q_copy(way, k).wait_send()
    for stage in (1, 2, 3):
        kv_stage(stage, lambda c: c.wait_send())
        w_stage(stage, lambda c: c.wait_send())
    for c in range(2):
        for i in range(1, nz):
            o_copy(c, i).wait_send()
            l_copy(c, i).wait_send()
            a_copy(c, i).wait_send()

    for c in range(2):
        tot = psend[c, t].astype(F32)
        for e in range(1, nt):
            p_copy(c, e).wait_recv()
            tot = tot + precv[c, e].astype(F32)
        tot = tot.astype(BF16)
        for j in range(NY):
            fsend[c, j] = tot[:, j * cols : (j + 1) * cols]
        for e in range(1, NY):
            f_copy(c, e).start()
        frecv[c, y] = fsend[c, y]
    for c in range(2):
        for e in range(1, NY):
            f_copy(c, e).wait_recv()
        for j in range(NY):
            out_ref[j * rows + c * half : j * rows + (c + 1) * half, :] = frecv[c, j]

    for c in range(2):
        for e in range(1, nt):
            p_copy(c, e).wait_send()
        for e in range(1, NY):
            f_copy(c, e).wait_send()


def body(nz, q, pk, pv, nk, nv, ck, cv, rr, cl, w):
    rows = q.shape[0]
    feat = q.shape[1]
    keys = pk.shape[0]
    reqs, slots = ck.shape[0], ck.shape[1]
    depth, cols = w.shape
    m = rows * QPG
    wide = NY * cols
    last = nz // 2
    vm = pltpu.VMEM
    dma = pltpu.SemaphoreType.DMA
    any_spec = pl.BlockSpec(memory_space=pl.ANY)
    vmem_spec = pl.BlockSpec(memory_space=pltpu.VMEM)
    return pl.pallas_call(
        functools.partial(kernel, nz),
        out_shape=jax.ShapeDtypeStruct((NY * rows, cols), BF16),
        in_specs=[any_spec] * 10,
        out_specs=vmem_spec,
        scratch_shapes=[
            vm((NY, keys, HD), BF16),
            vm((NY, keys, HD), BF16),
            vm((nz, rows, feat), BF16),
            vm((NY, depth, cols), BF16),
            vm((reqs, slots, HD), BF16),
            vm((reqs, slots, HD), BF16),
            vm((HD, HD), BF16),
            vm((HD, HD), BF16),
            pltpu.SMEM((rows,), jnp.int32),
            pltpu.SMEM((reqs,), jnp.int32),
            vm((2 * m, keys), F32),
            vm((2 * m, keys), F32),
            vm((nz, m, 2 * HD), F32),
            vm((nz, m, HD), F32),
            vm((2, nz, m // 2, HD), BF16),
            vm((2, nz, m // 2, HD), BF16),
            vm((2, nz, 1, HD), F32),
            vm((2, nz, 1, HD), F32),
            vm((2, nz, rows // 2, depth), BF16),
            vm((2, nz, rows // 2, wide), BF16),
            vm((2, nz, rows // 2, wide), BF16),
            vm((2, NY, rows // 2, cols), BF16),
            vm((2, NY, rows // 2, cols), BF16),
            dma((10,)),
            dma((2, last)),
            dma((2, last)),
            dma((12,)),
            dma((12,)),
            dma((6,)),
            dma((6,)),
            dma((2, nz)),
            dma((2, nz)),
            dma((2, nz)),
            dma((2, nz)),
            dma((2, nz)),
            dma((2, nz)),
            dma((2, nz)),
            dma((2, nz)),
            dma((2, NY)),
            dma((2, NY)),
        ],
        compiler_params=pltpu.CompilerParams(
            collective_id=0, has_side_effects=True, vmem_limit_bytes=60 * 1024 * 1024
        ),
    )(q, pk, pv, nk, nv, ck, cv, rr, cl, w)


def solution(mesh):
    nz = mesh.shape["seq"] // NY
    in_specs = (
        P("seq", "tp"),
        P("seq", "tp"),
        P("seq", "tp"),
        P("seq", "tp"),
        P("seq", "tp"),
        P("seq", None, "tp"),
        P("seq", None, "tp"),
        P("seq"),
        P("seq"),
        P("tp", "seq"),
    )
    return jax.shard_map(
        functools.partial(body, nz),
        mesh=mesh,
        in_specs=in_specs,
        out_specs=P("tp", "seq"),
        check_vma=False,
    )
```

```python
import functools
import math

import jax
import jax.numpy as jnp
from jax import lax
from jax.experimental import pallas as pl
from jax.experimental.pallas import tpu as pltpu
from jax.sharding import PartitionSpec as P

HD = 128
QPG = 8
NY = 4
MESH = pl.DeviceIdType.MESH
SCALE2 = math.log2(math.e) / math.sqrt(HD)
LOG2E = math.log2(math.e)
LOW = -1e30
F32 = jnp.float32
BF16 = jnp.bfloat16


def kernel(
    nz,
    q_ref,
    pk_ref,
    pv_ref,
    nk_ref,
    nv_ref,
    ck_ref,
    cv_ref,
    rr_ref,
    cl_ref,
    w_ref,
    out_ref,
    kbuf,
    vbuf,
    qbuf,
    wbuf,
    ckb,
    cvb,
    nkb,
    nvb,
    rrs,
    cls,
    sca,
    scb,
    acc,
    mst,
    osend,
    orecv,
    lsend,
    lrecv,
    att,
    psend,
    precv,
    fsend,
    frecv,
    loc_sem,
    qs,
    qr,
    ks,
    kr,
    ws,
    wr,
    os_,
    or_,
    ls,
    lr,
    as_,
    ar,
    ps,
    pr,
    fs,
    fr,
    heard,
):
    nt = nz
    rows = q_ref.shape[0]
    keys = pk_ref.shape[0]
    reqs, slots = ck_ref.shape[0], ck_ref.shape[1]
    depth, cols = w_ref.shape
    last = nz // 2
    s_idx = lax.axis_index("seq")
    t = lax.axis_index("tp")
    z = s_idx // NY
    y = s_idx % NY

    def at_z(v):
        return (lax.rem(v + 2 * nz, nz) * NY + y, t)

    def at_y(v):
        return (z * NY + lax.rem(v + 2 * NY, NY), t)

    def at_t(v):
        return (s_idx, lax.rem(v + 2 * nt, nt))

    def remote(src, dst, ssem, rsem, dev):
        return pltpu.make_async_remote_copy(
            src_ref=src,
            dst_ref=dst,
            send_sem=ssem,
            recv_sem=rsem,
            device_id=dev,
            device_id_type=MESH,
        )

    def greet(dev):
        pl.semaphore_signal(barrier, inc=1, device_id=dev, device_id_type=MESH)

    barrier = pltpu.get_barrier_semaphore()
    greet(at_y(y + 1))
    greet(at_y(y - 1))
    greet(at_z(z + 1))
    greet(at_z(z - 1))
    if nz == 8:
        greet(at_z(z + 2))
        greet(at_z(z - 2))
    partner = t + 1 - 2 * lax.rem(t, 2)
    greet(at_t(partner))
    if nt == 8:
        greet(at_t(t + 2))
        greet(at_t(t - 2))
        greet(at_t(partner + 4))

    local = [
        pltpu.make_async_copy(q_ref, qbuf.at[0], loc_sem.at[0]),
        pltpu.make_async_copy(ck_ref, ckb, loc_sem.at[1]),
        pltpu.make_async_copy(cv_ref, cvb, loc_sem.at[2]),
        pltpu.make_async_copy(nk_ref, nkb.at[pl.ds(0, rows)], loc_sem.at[3]),
        pltpu.make_async_copy(nv_ref, nvb.at[pl.ds(0, rows)], loc_sem.at[4]),
        pltpu.make_async_copy(rr_ref, rrs, loc_sem.at[5]),
        pltpu.make_async_copy(cl_ref, cls, loc_sem.at[6]),
        pltpu.make_async_copy(pk_ref, kbuf.at[0], loc_sem.at[7]),
        pltpu.make_async_copy(pv_ref, vbuf.at[0], loc_sem.at[8]),
        pltpu.make_async_copy(w_ref, wbuf.at[y], loc_sem.at[9]),
    ]
    pl.semaphore_wait(barrier, 10 if nz == 8 else 5)

    lo, hi = pl.ds(0, keys // 2), pl.ds(keys // 2, keys // 2)
    ways = (at_y(y + 1), at_y(y - 1))
    place = (lo, hi)

    def kv_copy(stage, way, which):
        buf = (kbuf, vbuf)[which]
        whole = (pk_ref, pv_ref)[which]
        sem = (stage - 1) * 4 + way * 2 + which
        if stage == 1:
            src = whole.at[place[way]]
        elif stage == 2:
            src = whole.at[place[1 - way]]
        else:
            src = buf.at[1, place[way]]
        return remote(src, buf.at[stage, place[way]], ks.at[sem], kr.at[sem], ways[way])

    def kv_stage(stage, act):
        for which in range(2):
            for way in range(2):
                act(kv_copy(stage, way, which))

    kv_stage(1, lambda c: c.start())

    half = rows // 2
    halves = (pl.ds(0, half), pl.ds(half, half))
    reach = 2 if nz == 8 else 1

    def q_slot(way, k):
        return 2 * k - 1 if (way == 0 or k == last) else 2 * k

    def q_copy(way, k):
        dst = qbuf.at[q_slot(way, k)]
        src = q_ref if k <= reach else qbuf.at[q_slot(way, reach)]
        step = k if k <= reach else k - reach
        if k == last:
            src, dst = src.at[halves[way]], dst.at[halves[way]]
        return remote(src, dst, qs.at[way, k - 1], qr.at[way, k - 1], at_z(z + step if way == 0 else z - step))

    for k in range(1, min(reach, last) + 1):
        for way in range(2):
            q_copy(way, k).start()
    for c in (local[0], local[7], local[8]):
        c.start()
    pl.semaphore_signal(heard, inc=1, device_id=at_t(partner), device_id_type=MESH)

    def queries_of(i, first=0, parts=2):
        return jnp.concatenate(
            [
                qbuf[i, c * half : (c + 1) * half, h * HD : (h + 1) * HD]
                for c in range(first, first + parts)
                for h in range(QPG)
            ],
            axis=0,
        )

    def per_head(bias):
        return jnp.concatenate([bias[:half]] * QPG + [bias[half:]] * QPG, axis=0)

    def scores(q, k):
        return lax.dot_general(q, k, (((1,), (1,)), ((), ())), preferred_element_type=F32)

    def with_ones(v):
        return jnp.concatenate([v, jnp.ones_like(v)], axis=1)

    for i in range(nz):
        acc[i] = jnp.zeros((rows * QPG, 2 * HD), F32)
        mst[i] = jnp.full((rows * QPG, HD), LOW, F32)

    mh = half * QPG

    def fill(buf, blk, picks):
        q = jnp.concatenate([queries_of(i, f, n) for i, f, n in picks], axis=0)
        buf[...] = scores(q, kbuf[blk])

    def absorb(buf, blk, picks):
        ws_, alphas = [], []
        at = 0
        for i, f, n in picks:
            m = n * mh
            own = pl.ds(f * mh, m)
            chunks = [buf[at : at + m, c * HD : (c + 1) * HD] for c in range(keys // HD)]
            at += m
            m_old = mst[i, own]
            m_new = jnp.maximum(
                m_old, functools.reduce(jnp.maximum, chunks).max(axis=1, keepdims=True)
            )
            m2 = m_new * SCALE2
            ws_.append(
                jnp.concatenate([jnp.exp2(c * SCALE2 - m2).astype(BF16) for c in chunks], axis=1)
            )
            alphas.append(jnp.exp2(m_old * SCALE2 - m2))
            mst[i, own] = m_new
        o = jnp.dot(
            jnp.concatenate(ws_, axis=0), with_ones(vbuf[blk]), preferred_element_type=F32
        )
        at = 0
        for (i, f, n), alpha in zip(picks, alphas):
            m = n * mh
            own = pl.ds(f * mh, m)
            acc[i, own] = acc[i, own] * jnp.concatenate([alpha, alpha], axis=1) + o[at : at + m]
            at += m

    late = max(last - 2, 0)
    early = list(range(late))
    order = [(0, p) for p in early[:2]] + [(1, p) for p in early[:2]]
    for p in early[2:]:
        order += [(0, p), (1, p)]
    tail = list(range(late, last))
    if tail:
        order += [(0, tail[0]), (1, tail[0])]
    order += [(2, p) for p in early + tail[:1]]
    for p in tail[1:]:
        order += [(0, p), (1, p), (2, p)]
    need_q = {}
    for n, (b, p) in enumerate(order):
        need_q.setdefault(p, n)
    need_b = {b: min(n for n, o in enumerate(order) if o[0] == b) for b in (0, 1, 2)}

    def waits(n):
        def when(cond, act):
            if isinstance(n, int):
                if n == cond:
                    act()
            else:
                pl.when(n == cond)(act)

        def q_step(k):
            for way in range(2):
                q_copy(way, k).wait_recv()
            if k == reach:
                for far in range(last, reach, -1):
                    for way in range(2):
                        q_copy(way, far).start()

        def own():
            for c in (local[0], local[7], local[8]):
                c.wait()

        def blk1():
            for which in range(2):
                for way in range(2):
                    kv_copy(1, way, which).wait_recv()
                    kv_copy(3, way, which).start()

        when(need_b[0], own)
        for p in range(last):
            when(need_q[p], lambda p=p: q_step(p + 1))
        when(need_b[1], blk1)
        when(need_b[2], lambda: kv_stage(2, lambda c: c.wait_recv()))

    def tile(n):
        if isinstance(n, int):
            b, p = order[n]
        else:
            b = p = 0
            for m, (bb, pp) in enumerate(order):
                b = jnp.where(n == m, bb, b)
                p = jnp.where(n == m, pp, p)
        return b, [(2 * p, 0, 2), (2 * p + 1, 0, 2)]

    count = len(order)
    waits(0)
    fill(sca, *tile(0))
    kv_stage(2, lambda c: c.start())
    for c in local[1:7] + local[9:]:
        c.start()

    def step(m, carry):
        for buf, other, n in ((sca, scb, 2 * m), (scb, sca, 2 * m + 1)):
            waits(n + 1)
            fill(other, *tile(n + 1))
            absorb(buf, *tile(n))
        return carry

    pairs = (count - 1) // 2
    lax.fori_loop(0, pairs, step, 0)
    rest = list(range(2 * pairs, count))
    bufs = (sca, scb)
    for n in rest:
        if n + 1 < count:
            waits(n + 1)
            fill(bufs[(n + 1) % 2], *tile(n + 1))
        absorb(bufs[n % 2], *tile(n))

    wlo, whi = pl.ds(0, depth // 2), pl.ds(depth // 2, depth // 2)
    wplace = (wlo, whi)
    origin = (lax.rem(y + NY - 1, NY), lax.rem(y + 1, NY))

    def w_copy(stage, way):
        sem = (stage - 1) * 2 + way
        if stage == 3:
            src = dst = wbuf.at[origin[way], wplace[way]]
        else:
            part = wplace[way] if stage == 1 else wplace[1 - way]
            src, dst = w_ref.at[part], wbuf.at[y, part]
        return remote(src, dst, ws.at[sem], wr.at[sem], ways[way])

    def w_stage(stage, act):
        for way in range(2):
            act(w_copy(stage, way))

    lane8 = lax.broadcasted_iota(jnp.int32, (8, HD), 1)
    groups = half // 8

    staged = nz == 8

    def o_dest(c, i):
        if staged and i == 7:
            return at_z(z - 2) if c == 0 else at_z(z + 2)
        if staged and i > 4:
            return at_z(z - 1) if i == 5 else at_z(z + 1)
        return at_z(z - (i + 1) // 2) if i % 2 else at_z(z + i // 2)

    def o_copy(c, i):
        return remote(osend.at[c, i], orecv.at[c, i], os_.at[c, i], or_.at[c, i], o_dest(c, i))

    def l_copy(c, i):
        return remote(lsend.at[c, i], lrecv.at[c, i], ls.at[c, i], lr.at[c, i], o_dest(c, i))

    def o_start(c, i):
        o_copy(c, i).start()
        l_copy(c, i).start()

    def o_wait(c, i):
        o_copy(c, i).wait_recv()
        l_copy(c, i).wait_recv()

    def finish(c, i):
        own = pl.ds(c * mh, mh)
        a = acc[i, own]
        l = a[:, HD:]
        osend[c, i] = (a[:, :HD] / l).astype(BF16)
        m = mst[i, own]
        top_of = jnp.zeros((8, HD), F32)
        sum_of = jnp.ones((8, HD), F32)
        for h in range(QPG):
            for g in range(groups):
                r0 = h * half + g * 8
                pick = lane8 == g * 8 + h
                top_of = jnp.where(pick, m[r0 : r0 + 8, :], top_of)
                sum_of = jnp.where(pick, l[r0 : r0 + 8, :], sum_of)
        packed = top_of * SCALE2 + jnp.log(sum_of) * LOG2E
        rolled = pltpu.roll(packed, 0, 1, stride=16, stride_axis=0)
        lsend[c, i] = jnp.sum(rolled, axis=0, keepdims=True)

    finals = []
    for top_slot, low_slot in ((nz, nz // 2), (nz // 2, 0)):
        for c in range(2):
            finals.append((c, [(i, c, 1) for i in range(top_slot - 1, low_slot - 1, -1)]))

    def part(n):
        return (sca, scb)[n % 2].at[pl.ds(0, len(finals[n][1]) * mh)]

    for way in range(2):
        kv_copy(3, way, 0).wait_recv()
    fill(part(0), 3, finals[0][1])
    for way in range(2):
        kv_copy(3, way, 1).wait_recv()
    for n, (c, picks) in enumerate(finals):
        if n + 1 < len(finals):
            fill(part(n + 1), 3, finals[n + 1][1])
        absorb(part(n), 3, picks)
        for i, _, _ in picks:
            if i > 0:
                finish(c, i)
                if not (staged and i in (3, 4)):
                    o_start(c, i)
        if n == 0:
            w_stage(1, lambda c: c.start())
        if n == 2:
            w_stage(2, lambda c: c.start())

    pad = nkb.shape[0]
    nkb[pl.ds(rows, pad - rows), :] = jnp.zeros((pad - rows, HD), BF16)
    nvb[pl.ds(rows, pad - rows), :] = jnp.zeros((pad - rows, HD), BF16)
    for c in local[1:7]:
        c.wait()
    sub = lax.broadcasted_iota(jnp.int32, (rows, pad), 0)
    lane = lax.broadcasted_iota(jnp.int32, (rows, pad), 1)
    rr_col = jnp.zeros((rows, pad), jnp.int32)
    rr_row = jnp.zeros((rows, pad), jnp.int32)
    for r in range(rows):
        req = rrs[r] - s_idx * reqs
        rr_col = jnp.where(sub == r, req, rr_col)
        rr_row = jnp.where(lane == r, req, rr_row)

    q_own = queries_of(0)
    parts = []
    for j in range(reqs):
        biases = [
            jnp.where((rr_col == j) & (lane + c * pad < cls[j]), 0.0, LOW).astype(F32)
            for c in range(slots // pad)
        ]
        bias = jnp.concatenate(biases, axis=1)
        parts.append(scores(q_own, ckb[j]) + per_head(bias))
    bias = jnp.where((rr_row == rr_col) & (lane <= sub), 0.0, LOW).astype(F32)
    parts.append(scores(q_own, nkb[...]) + per_head(bias))
    top = functools.reduce(jnp.maximum, [p.max(axis=1, keepdims=True) for p in parts])
    total = jnp.zeros((rows * QPG, 2 * HD), F32)
    for j, p in enumerate(parts):
        w = jnp.exp2((p - top) * SCALE2).astype(BF16)
        v = cvb[j] if j < reqs else nvb[...]
        total = total + jnp.dot(w, with_ones(v), preferred_element_type=F32)
    top = jnp.broadcast_to(top, (rows * QPG, HD))
    m_old = mst[0]
    m_new = jnp.maximum(m_old, top)
    keep = jnp.exp2((m_old - m_new) * SCALE2)
    add = jnp.exp2((top - m_new) * SCALE2)
    acc[0] = acc[0] * jnp.concatenate([keep, keep], axis=1) + total * jnp.concatenate(
        [add, add], axis=1
    )
    mst[0] = m_new
    for c in range(2):
        finish(c, 0)

    far_first = sorted(range(1, nz), key=lambda d: -min(d, nz - d))

    def a_copy(c, d):
        ref = att.at[c, z]
        return remote(ref, ref, as_.at[c, d], ar.at[c, d], at_z(z + d))

    sub8 = lax.broadcasted_iota(jnp.int32, (8, HD), 0)

    def spread(row):
        row = jnp.broadcast_to(row, (8, HD))
        out = row
        for k in range(1, 8):
            out = jnp.where(sub8 == k, pltpu.roll(row, HD - 16 * k, 1), out)
        return out

    def weights(c, sources):
        lses = [lsend[c, i] if own else lrecv[c, i] for own, i in sources]
        best = functools.reduce(jnp.maximum, lses)
        wts = [jnp.exp2(v - best) for v in lses]
        norm = functools.reduce(jnp.add, wts)
        return [spread(v / norm) for v in wts], best + jnp.log(norm) * LOG2E

    def blend(c, sources, wts, h):
        tot = jnp.zeros((half, HD), F32)
        for (own, i), w in zip(sources, wts):
            o = (osend if own else orecv)[c, i, h * half : (h + 1) * half, :].astype(F32)
            col = jnp.concatenate(
                [w[:, g * 8 + h : g * 8 + h + 1] for g in range(groups)], axis=0
            )
            tot = tot + o * col
        return tot.astype(BF16)

    def join(c):
        for i in (4 - c, 3 + c):
            sources = [(True, i), (False, i + 2)]
            if i == 3 + c:
                sources.append((False, 7))
            for _, extra in sources[1:]:
                o_wait(c, extra)
            wts, lse = weights(c, sources)
            for h in range(QPG):
                osend[c, i, h * half : (h + 1) * half, :] = blend(c, sources, wts, h)
            lsend[c, i] = lse
            o_start(c, i)

    def merge(c):
        arriving = range(1, 5) if staged else range(1, nz)
        for i in arriving:
            o_wait(c, i)
        sources = [(True, 0)] + [(False, i) for i in arriving]
        wts, _ = weights(c, sources)
        for h in range(QPG):
            att[c, z, :, h * HD : (h + 1) * HD] = blend(c, sources, wts, h)
        for d in far_first:
            a_copy(c, d).start()

    if staged:
        join(0)
        join(1)
    merge(0)
    merge(1)
    pl.semaphore_wait(heard, 1)
    w_stage(1, lambda c: c.wait_recv())
    w_stage(3, lambda c: c.start())

    local[9].wait()
    w_stage(2, lambda c: c.wait_recv())
    w_stage(3, lambda c: c.wait_recv())

    def p_copy(c, e):
        dst_t = lax.rem(t + e, nt)
        return remote(psend.at[c, dst_t], precv.at[c, e], ps.at[c, e], pr.at[c, e], at_t(t + e))

    for c in range(2):
        for d in far_first:
            a_copy(c, d).wait_recv()
        a_all = att[c].reshape(nz * half, depth)
        for j in range(NY):
            out = jnp.dot(a_all, wbuf[j], preferred_element_type=F32).astype(BF16)
            psend[c, :, :, j * cols : (j + 1) * cols] = out.reshape(nz, half, cols)
        for e in sorted(range(1, nt), key=lambda e: -min(e, nt - e)):
            p_copy(c, e).start()

    def f_copy(c, e):
        dst_y = lax.rem(y + e, NY)
        return remote(fsend.at[c, dst_y], frecv.at[c, y], fs.at[c, e], fr.at[c, e], at_y(y + e))

    for way in range(2):
        for k in range(1, last + 1):
            q_copy(way, k).wait_send()
    for stage in (1, 2, 3):
        kv_stage(stage, lambda c: c.wait_send())
        w_stage(stage, lambda c: c.wait_send())
    for c in range(2):
        for i in range(1, nz):
            o_copy(c, i).wait_send()
            l_copy(c, i).wait_send()
            a_copy(c, i).wait_send()

    for c in range(2):
        tot = psend[c, t].astype(F32)
        for e in range(1, nt):
            p_copy(c, e).wait_recv()
            tot = tot + precv[c, e].astype(F32)
        tot = tot.astype(BF16)
        for j in range(NY):
            fsend[c, j] = tot[:, j * cols : (j + 1) * cols]
        for e in range(1, NY):
            f_copy(c, e).start()
        frecv[c, y] = fsend[c, y]
    for c in range(2):
        for e in range(1, NY):
            f_copy(c, e).wait_recv()
        for j in range(NY):
            out_ref[j * rows + c * half : j * rows + (c + 1) * half, :] = frecv[c, j]

    for c in range(2):
        for e in range(1, nt):
            p_copy(c, e).wait_send()
        for e in range(1, NY):
            f_copy(c, e).wait_send()


def body(nz, q, pk, pv, nk, nv, ck, cv, rr, cl, w):
    rows = q.shape[0]
    feat = q.shape[1]
    keys = pk.shape[0]
    reqs, slots = ck.shape[0], ck.shape[1]
    depth, cols = w.shape
    m = rows * QPG
    wide = NY * cols
    last = nz // 2
    vm = pltpu.VMEM
    dma = pltpu.SemaphoreType.DMA
    any_spec = pl.BlockSpec(memory_space=pl.ANY)
    vmem_spec = pl.BlockSpec(memory_space=pltpu.VMEM)
    return pl.pallas_call(
        functools.partial(kernel, nz),
        out_shape=jax.ShapeDtypeStruct((NY * rows, cols), BF16),
        in_specs=[any_spec] * 10,
        out_specs=vmem_spec,
        scratch_shapes=[
            vm((NY, keys, HD), BF16),
            vm((NY, keys, HD), BF16),
            vm((nz, rows, feat), BF16),
            vm((NY, depth, cols), BF16),
            vm((reqs, slots, HD), BF16),
            vm((reqs, slots, HD), BF16),
            vm((HD, HD), BF16),
            vm((HD, HD), BF16),
            pltpu.SMEM((rows,), jnp.int32),
            pltpu.SMEM((reqs,), jnp.int32),
            vm((2 * m, keys), F32),
            vm((2 * m, keys), F32),
            vm((nz, m, 2 * HD), F32),
            vm((nz, m, HD), F32),
            vm((2, nz, m // 2, HD), BF16),
            vm((2, nz, m // 2, HD), BF16),
            vm((2, nz, 1, HD), F32),
            vm((2, nz, 1, HD), F32),
            vm((2, nz, rows // 2, depth), BF16),
            vm((2, nz, rows // 2, wide), BF16),
            vm((2, nz, rows // 2, wide), BF16),
            vm((2, NY, rows // 2, cols), BF16),
            vm((2, NY, rows // 2, cols), BF16),
            dma((10,)),
            dma((2, last)),
            dma((2, last)),
            dma((12,)),
            dma((12,)),
            dma((6,)),
            dma((6,)),
            dma((2, nz)),
            dma((2, nz)),
            dma((2, nz)),
            dma((2, nz)),
            dma((2, nz)),
            dma((2, nz)),
            dma((2, nz)),
            dma((2, nz)),
            dma((2, NY)),
            dma((2, NY)),
            pltpu.SemaphoreType.REGULAR,
        ],
        compiler_params=pltpu.CompilerParams(
            collective_id=0, has_side_effects=True, vmem_limit_bytes=60 * 1024 * 1024
        ),
    )(q, pk, pv, nk, nv, ck, cv, rr, cl, w)


def solution(mesh):
    nz = mesh.shape["seq"] // NY
    in_specs = (
        P("seq", "tp"),
        P("seq", "tp"),
        P("seq", "tp"),
        P("seq", "tp"),
        P("seq", "tp"),
        P("seq", None, "tp"),
        P("seq", None, "tp"),
        P("seq"),
        P("seq"),
        P("tp", "seq"),
    )
    return jax.shard_map(
        functools.partial(body, nz),
        mesh=mesh,
        in_specs=in_specs,
        out_specs=P("tp", "seq"),
        check_vma=False,
    )
```
